32 devices in a mesh: groups: 2 (over y), seq: 8 (over z, core), dp: 2 (over x).
Axes of the slice: x: 2, y: 2, z: 4, core: 2. Of those that a mesh axis runs over, the one named last changes fastest.
Arguments:
- tokens: bfloat16 [4, 1024, 1024], P(('groups', 'dp'), 'seq'), parts along dimension 0, may hold values from -6 to 6
- w_query: bfloat16 [1024, 1024], replicated, may hold values from -0.1875 to 0.1875
- w_key: bfloat16 [1024, 1024], replicated, may hold values from -0.1875 to 0.1875
- w_value: bfloat16 [1024, 1024], replicated, may hold values from -0.1875 to 0.1875
- w_output: bfloat16 [1024, 1024], replicated, may hold values from -0.1875 to 0.1875
- out_cotangent: bfloat16 [4, 1024, 1024], P(('groups', 'dp'), 'seq'), parts along dimension 0, may hold values from -6 to 6
Outputs:
- attended: bfloat16 [4, 1024, 1024], P(('groups', 'dp'), 'seq'), parts along dimension 0
- d_tokens: bfloat16 [4, 1024, 1024], P(('groups', 'dp'), 'seq'), parts along dimension 0
- weight_grads: float32 [2048, 4096], P(('groups', 'seq', 'dp')), parts along dimension 0
The draws below stay inside these ranges and needn't reach their ends.
There are 2 independent parts, one for each index of `groups`. The reference program is written for one: setup_inputs(seed, part) draws one part's arguments, and reference() takes and returns one part's arrays. A program takes and returns all parts, laid end to end along the dimension named above; an argument that names none is the same for every part. Nothing has to cross between parts.
All inputs are finite; a program needn't handle non-finite values.
Results may differ from the reference program's by a relative error of at most 0.008.
Values sent between devices are 32-bit elements; how exact they have to be, the bound alone decides.
A program may use at most 128 MiB of HBM per device.

```python
import math
import jax
import jax.numpy as jnp
from jax import lax

D = 1024
H = 8
DH = 128
TOK_DEV = 128
CLIPS = 2
LENGTH = 1024
N_SEQ = 8


def spiked(values, stream_key, source, target, parts, factor):
    owner, partner = [(jnp.arange(values.shape[axis_at]) // (values.shape[axis_at] // parts)).reshape([-1 if axis == axis_at else 1 for axis in range(values.ndim)]) for axis_at in (source, target)]
    chosen = jax.random.permutation(stream_key, parts)[partner]
    strong = (owner == chosen) | (owner == (partner + parts // 2) % parts)
    return jnp.where(strong, factor * values, values)


def levels(key, shape, shards, least, high):
    def one(dim, parts):
        draws = jax.random.uniform(jax.random.fold_in(jax.random.fold_in(key, 6), dim), (parts,), jnp.float32, least / len(shards), high / len(shards))
        return jnp.repeat(jnp.exp(draws), shape[dim] // parts).reshape((-1,) + (1,) * (len(shape) - dim - 1))

    gain = one(*shards[0])
    for cut in shards[1:]:
        gain = gain * one(*cut)
    return gain


def noise(own_key, dims, spread, most, split=(), dtype=jnp.bfloat16):
    values = jax.random.normal(own_key, dims, jnp.float32) * spread
    if len(split) > 0:
        values = levels(own_key, dims, split, -0.22, 0.18) * values
    return jnp.clip(values, min=-most, max=most).astype(dtype)


def heavy_noise(rng, shape, scale, bound, cuts, heavy, held_as=jnp.bfloat16):
    values = scale * jax.random.normal(rng, shape, jnp.float32)
    if cuts:
        values = values * levels(rng, shape, cuts, -0.22, 0.18)
    return jnp.clip(spiked(values, jax.random.fold_in(rng, 3), *heavy), -bound, bound).astype(held_as)


def setup_inputs(seed: int = 0, part: int = 0) -> dict:
    splits = jax.random.split(jax.random.key(seed), 7)
    part_splits = jax.random.split(jax.random.fold_in(splits[6], part), 7)
    tokens = heavy_noise(part_splits[0], (CLIPS, LENGTH, D), 1.0, 6.0, ((0, 2), (1, 8)), (1, 2, 8, 2.0))
    w_query = noise(splits[1], (D, D), D ** -0.5, 0.1875)
    w_key = noise(splits[2], (D, D), D ** -0.5, 0.1875)
    w_value = noise(splits[3], (D, D), D ** -0.5, 0.1875)
    w_output = noise(splits[4], (D, D), D ** -0.5, 0.1875)
    out_cotangent = noise(part_splits[5], (CLIPS, LENGTH, D), 1.0, 6.0, ((0, 2), (1, 8)))
    return dict(tokens=tokens, w_query=w_query, w_key=w_key, w_value=w_value, w_output=w_output, out_cotangent=out_cotangent)


EPSILON = 1e-05

def to_blocks(array):
    clip_count = array.shape[0]
    return array.reshape(clip_count, N_SEQ, TOK_DEV, H, DH).transpose(1, 0, 2, 3, 4)

def from_blocks(array):
    clip_count = array.shape[1]
    return array.transpose(1, 0, 2, 3, 4).reshape(clip_count, N_SEQ * TOK_DEV, H * DH)

def causal_mask(row_count):
    rows = lax.broadcasted_iota(jnp.int32, (row_count, row_count), 0)
    cols = lax.broadcasted_iota(jnp.int32, (row_count, row_count), 1)
    return rows >= cols

def project(flattened, weight):
    return jnp.dot(flattened, weight, preferred_element_type=jnp.float32).astype(jnp.bfloat16)

def forward_block(operands):
    queries, key_rows, value_rows, carried = operands
    causal = causal_mask(queries.shape[1])
    scores = jnp.einsum('cthd,cshd->chts', queries.astype(jnp.float32), key_rows.astype(jnp.float32))
    attn_weights = jnp.where(causal, scores, 0.0).astype(jnp.bfloat16)
    local_part = jnp.einsum('chts,cshd->cthd', attn_weights.astype(jnp.float32), value_rows.astype(jnp.float32))
    carried_part = jnp.einsum('cthd,chde->cthe', queries.astype(jnp.float32), carried.astype(jnp.float32))
    return local_part + carried_part

def backward_block(operands):
    queries, key_rows, value_rows, carried, later, d_heads = operands
    causal = causal_mask(queries.shape[1])
    qf = queries.astype(jnp.float32)
    kf = key_rows.astype(jnp.float32)
    vf = value_rows.astype(jnp.float32)
    gf = d_heads.astype(jnp.float32)
    cf = carried.astype(jnp.float32)
    lf = later.astype(jnp.float32)
    scores = jnp.einsum('cthd,cshd->chts', qf, kf)
    attn_weights = jnp.where(causal, scores, 0.0).astype(jnp.bfloat16).astype(jnp.float32)
    back_scores = jnp.where(causal, jnp.einsum('cthe,cshe->chts', gf, vf), 0.0).astype(jnp.bfloat16).astype(jnp.float32)
    d_query = jnp.einsum('chts,cshd->cthd', back_scores, kf) + jnp.einsum('cthe,chde->cthd', gf, cf)
    d_key = jnp.einsum('chts,cthd->cshd', back_scores, qf) + jnp.einsum('cshe,chde->cshd', vf, lf)
    d_value = jnp.einsum('chts,cthe->cshe', attn_weights, gf) + jnp.einsum('cshd,chde->cshe', kf, lf)
    return (d_query.astype(jnp.bfloat16), d_key.astype(jnp.bfloat16), d_value.astype(jnp.bfloat16))

def reference(tokens, w_query, w_key, w_value, w_output, out_cotangent):
    clip_count = tokens.shape[0]
    flattened = tokens.reshape(-1, D)
    queries = to_blocks(project(flattened, w_query).reshape(clip_count, LENGTH, D))
    key_rows = to_blocks(project(flattened, w_key).reshape(clip_count, LENGTH, D))
    value_rows = to_blocks(project(flattened, w_value).reshape(clip_count, LENGTH, D))
    states = jnp.einsum('bcshd,bcshe->bchde', key_rows.astype(jnp.float32), value_rows.astype(jnp.float32))
    zero_state = jnp.zeros_like(states[:1])
    carried = jnp.concatenate([zero_state, jnp.cumsum(states, axis=0)[:-1]], axis=0).astype(jnp.bfloat16)
    mixed = from_blocks(lax.map(forward_block, (queries, key_rows, value_rows, carried)))
    scale_rows = jnp.sqrt(lax.optimization_barrier(jnp.mean(mixed * mixed, axis=-1, keepdims=True)) + EPSILON)
    normed = mixed / scale_rows
    normed_bf = normed.astype(jnp.bfloat16)
    normed_flat = normed_bf.reshape(-1, D)
    attended = jnp.dot(normed_flat, w_output, preferred_element_type=jnp.float32).astype(jnp.bfloat16)
    attended = attended.reshape(clip_count, LENGTH, D)
    cot_flat = out_cotangent.reshape(-1, D)
    back_norm = jnp.dot(cot_flat, w_output.T, preferred_element_type=jnp.float32).reshape(clip_count, LENGTH, D)
    d_mixed = ((back_norm - normed * lax.optimization_barrier(jnp.mean(back_norm * normed, axis=-1, keepdims=True))) / scale_rows).astype(jnp.bfloat16)
    d_heads = to_blocks(d_mixed)
    back_states = jnp.einsum('bcthd,bcthe->bchde', queries.astype(jnp.float32), d_heads.astype(jnp.float32))
    reversed_sums = jnp.cumsum(back_states[::-1], axis=0)[::-1]
    later = jnp.concatenate([reversed_sums[1:], zero_state], axis=0).astype(jnp.bfloat16)
    d_query, d_key, d_value = lax.map(backward_block, (queries, key_rows, value_rows, carried, later, d_heads))
    d_query = from_blocks(d_query).reshape(-1, D)
    d_key = from_blocks(d_key).reshape(-1, D)
    d_value = from_blocks(d_value).reshape(-1, D)
    d_tokens = jnp.dot(d_query, w_query.T, preferred_element_type=jnp.float32)
    d_tokens = d_tokens + jnp.dot(d_key, w_key.T, preferred_element_type=jnp.float32)
    d_tokens = d_tokens + jnp.dot(d_value, w_value.T, preferred_element_type=jnp.float32)
    d_tokens = d_tokens.astype(jnp.bfloat16).reshape(clip_count, LENGTH, D)
    grad_query = jnp.dot(flattened.T, d_query, preferred_element_type=jnp.float32)
    grad_key = jnp.dot(flattened.T, d_key, preferred_element_type=jnp.float32)
    grad_value = jnp.dot(flattened.T, d_value, preferred_element_type=jnp.float32)
    grad_output = jnp.dot(normed_flat.T, cot_flat, preferred_element_type=jnp.float32)
    factor = 1.0 / math.sqrt(CLIPS * LENGTH)
    weight_grads = jnp.concatenate([grad_query, grad_key, grad_value, grad_output], axis=1) * factor
    return (attended, d_tokens, weight_grads)
```

```python
import functools
import math

import jax
import jax.numpy as jnp
from jax import lax
from jax.experimental import pallas as pl
from jax.experimental.pallas import tpu as pltpu
from jax.sharding import PartitionSpec as P

H = 8
EPSILON = 1e-05
MESH = pl.DeviceIdType.MESH
F32, BF16 = jnp.float32, jnp.bfloat16
COLUMN_BLOCK = (3, 0, 1, 2)


def mm(a, b, ca, cb):
    return lax.dot_general(a, b, (((ca,), (cb,)), ((), ())), preferred_element_type=F32)


def kernel(
    n_seq, m,
    tok_ref, cot_ref, wq_hbm, wk_hbm, wv_hbm, wo_hbm,
    att_ref, dtok_ref, wg_ref,
    wq, wk, wv, wo,
    q_s, k_s, v_s, attn_s, mixed_s, back_s, carried_s, later_s, dm_s, nb_s, dqkv_s,
    gbuf, xt, xland, lhs, part, inb, sown, spart, crecv, csend,
    w_sem, g_send, g_fwd, g_recv, x_send, x_recv, e_send, e_recv,
    c_send, c_recv, p_send, p_recv, r_send, r_recv,
):
    t_rows, width = tok_ref.shape
    dh = width // H
    half = H // 2
    n_z = n_seq // 2
    rows = wg_ref.shape[0]
    members = 2 * m
    s, d = lax.axis_index("seq"), lax.axis_index("dp")
    z, c = lax.div(s, 2), lax.rem(s, 2)
    me = c * m + d
    up, down = z < n_z - 1, z > 0
    partner = {"seq": 2 * z + 1 - c, "dp": d}
    above = {"seq": jnp.minimum(s + 2, n_seq - 2 + c), "dp": d}
    below = {"seq": jnp.maximum(s - 2, c), "dp": d}
    pending = []

    def rcopy(src, dst, ss, rs, dev):
        return pltpu.make_async_remote_copy(
            src_ref=src, dst_ref=dst, send_sem=ss, recv_sem=rs,
            device_id=dev, device_id_type=MESH,
        )

    def arrived(ref, sem):
        rcopy(ref, ref, w_sem.at[0], sem, partner).wait_recv()

    loads = [
        pltpu.make_async_copy(src, dst, w_sem.at[i])
        for i, (src, dst) in enumerate(
            ((wk_hbm, wk), (wv_hbm, wv), (wq_hbm, wq), (wo_hbm, wo))
        )
    ]
    for load in loads:
        load.start()

    def member(rel):
        t = lax.rem(me + rel, members)
        return t, lax.div(t, m), lax.rem(t, m)

    barrier = pltpu.get_barrier_semaphore()
    for rel in range(1, members):
        _, tc, td = member(rel)
        pl.semaphore_signal(
            barrier, inc=1, device_id={"seq": 2 * z + tc, "dp": td}, device_id_type=MESH
        )

    @pl.when(up)
    def _():
        pl.semaphore_signal(barrier, inc=1, device_id=above, device_id_type=MESH)

    @pl.when(down)
    def _():
        pl.semaphore_signal(barrier, inc=1, device_id=below, device_id_type=MESH)

    pl.semaphore_wait(
        barrier, members - 1 + jnp.where(up, 1, 0) + jnp.where(down, 1, 0)
    )

    def gather_start(k, value):
        gbuf[k, me] = value
        own = gbuf.at[k, me]
        first = rcopy(own, own, g_send.at[k, 0], g_recv.at[k, me], partner)
        first.start()
        pending.append((None, first))
        for j in range(1, m):
            to = {"seq": s, "dp": lax.rem(d + j, m)}
            copy = rcopy(own, own, g_send.at[k, j], g_recv.at[k, me], to)
            copy.start()
            pending.append((None, copy))

    def gather_forward(k):
        for j in range(1, m):
            slot = c * m + lax.rem(d + m - j, m)
            ref = gbuf.at[k, slot]
            arrived(ref, g_recv.at[k, slot])
            copy = rcopy(ref, ref, g_fwd.at[k, j], g_recv.at[k, slot], partner)
            copy.start()
            pending.append((None, copy))

    def gather_finish(k):
        for j in range(m):
            slot = (1 - c) * m + j
            arrived(gbuf.at[k, slot], g_recv.at[k, slot])

    def columns_start(kind, value):
        xt[kind] = value.T.reshape(n_z, 2, m, rows, t_rows)
        xland[kind, me] = xt[kind, :, c, d]
        for rel in range(1, members):
            t, tc, td = member(rel)
            copy = rcopy(
                xt.at[kind, :, tc, td], xland.at[kind, me], x_send.at[kind, rel],
                x_recv.at[kind, me], {"seq": 2 * z + tc, "dp": td},
            )
            copy.start()
            pending.append((None, copy))

    def columns_finish(kind):
        for rel in range(1, members):
            t, _, _ = member(rel)
            arrived(xland.at[kind, t], x_recv.at[kind, t])
        for j in range(members):
            lhs[kind, :, j * t_rows:(j + 1) * t_rows] = (
                xland[kind, j].reshape(n_z * rows, t_rows).astype(BF16)
            )

    def exchange_start(way):
        copy = rcopy(sown.at[way], spart.at[way], e_send.at[way], e_recv.at[way], partner)
        copy.start()
        pending.append((None, copy))

    def chain(way):
        has_in, has_out, to = (down, up, above) if way == 0 else (up, down, below)
        arrived(spart.at[way], e_recv.at[way])

        @pl.when(jnp.logical_not(has_in))
        def _():
            crecv[way] = jnp.zeros(crecv.shape[1:], F32)

        for j in range(half):
            h = c * half + j
            ref = crecv.at[way, h]
            side = rcopy(ref, ref, p_send.at[way, j], p_recv.at[way, j], partner)
            ahead = rcopy(csend.at[way, j], ref, c_send.at[way, j], c_recv.at[way, j], to)

            @pl.when(has_in)
            def _():
                arrived(ref, c_recv.at[way, j])

            @pl.when(has_out)
            def _():
                csend[way, j] = crecv[way, h] + (sown[way, h] + spart[way, h])
                ahead.start()

            @pl.when(has_in)
            def _():
                side.start()

            pending.append((has_in, side))
            pending.append((has_out, ahead))

    def chain_finish(way, out):
        has_in = down if way == 0 else up
        for j in range(half):
            @pl.when(has_in)
            def _():
                arrived(crecv.at[way, (1 - c) * half + j], p_recv.at[way, j])

        takes = c == 1 - way
        for h in range(H):
            out[h] = jnp.where(
                takes, crecv[way, h] + spart[way, h], crecv[way, h]
            ).astype(BF16)

    def block_up(k, zp):
        ref = part.at[k, zp]
        return rcopy(ref, inb.at[k, zp], r_send.at[k, zp], r_recv.at[k, zp], above)

    def block_down(k, zp):
        slot = jnp.where(zp == z - 1, n_z, zp)
        return rcopy(
            part.at[k, zp], inb.at[k, slot], r_send.at[k, zp], r_recv.at[k, slot], below
        )

    def partial(k):
        right = gbuf[k].reshape(members * t_rows, width).astype(BF16)
        left = lhs[1 if k == 0 else 0]
        part[k] = mm(left, right, 1, 0).reshape(n_z, rows, width)

        @pl.when(z == 0)
        def _():
            for zp in reversed(range(1, n_z)):
                block_up(k, zp).start()

        @pl.when(z == n_z - 1)
        def _():
            for zp in range(n_z - 1):
                block_down(k, zp).start()

    def pass_on(k):
        for step in range(n_z - 1):
            high, low = n_z - 1 - step, step

            @pl.when((z > 0) & (z < high))
            def _():
                arrived(inb.at[k, high], r_recv.at[k, high])
                part[k, high] = part[k, high] + inb[k, high]
                block_up(k, high).start()

            @pl.when((z < n_z - 1) & (z > low))
            def _():
                arrived(inb.at[k, low], r_recv.at[k, low])
                part[k, low] = part[k, low] + inb[k, low]
                block_down(k, low).start()

    token_total = t_rows * n_seq * m

    def finish(k):
        @pl.when(down)
        def _():
            arrived(inb.at[k, z], r_recv.at[k, z])
            part[k, z] = part[k, z] + inb[k, z]

        @pl.when(up)
        def _():
            arrived(inb.at[k, n_z], r_recv.at[k, n_z])
            part[k, z] = part[k, z] + inb[k, n_z]

        at = COLUMN_BLOCK[k] * width
        wg_ref[:, at:at + width] = part[k, z] * (1.0 / math.sqrt(token_total))

    def head(h):
        return slice(h * dh, (h + 1) * dh)

    loads[0].wait()
    k_s[...] = mm(tok_ref[...], wk[...], 1, 0).astype(BF16)
    loads[1].wait()
    v_s[...] = mm(tok_ref[...], wv[...], 1, 0).astype(BF16)
    for h in range(H):
        sown[0, h] = mm(k_s[:, head(h)], v_s[:, head(h)], 0, 0)
    exchange_start(0)
    gather_start(0, cot_ref[...].astype(F32))
    loads[2].wait()
    q_s[...] = mm(tok_ref[...], wq[...], 1, 0).astype(BF16)
    chain(0)
    columns_start(0, tok_ref[...].astype(F32))
    loads[3].wait()
    back_s[...] = mm(cot_ref[...], wo[...], 1, 1)
    causal = lax.broadcasted_iota(jnp.int32, (t_rows, t_rows), 0) >= (
        lax.broadcasted_iota(jnp.int32, (t_rows, t_rows), 1)
    )
    for h in range(H):
        scores = mm(q_s[:, head(h)], k_s[:, head(h)], 1, 1)
        weights = jnp.where(causal, scores, 0.0).astype(BF16)
        attn_s[h] = weights
        mixed_s[:, head(h)] = mm(weights, v_s[:, head(h)], 1, 0)
    chain_finish(0, carried_s)
    for h in range(H):
        mixed_s[:, head(h)] += mm(q_s[:, head(h)], carried_s[h], 1, 0)

    mixed = mixed_s[...]
    scale_rows = jnp.sqrt(jnp.mean(mixed * mixed, axis=-1, keepdims=True) + EPSILON)
    normed = mixed / scale_rows
    nb_s[...] = normed.astype(BF16)
    back = back_s[...]
    dm_s[...] = (
        (back - normed * jnp.mean(back * normed, axis=-1, keepdims=True)) / scale_rows
    ).astype(BF16)
    for h in range(H):
        sown[1, h] = mm(q_s[:, head(h)], dm_s[:, head(h)], 0, 0)
    exchange_start(1)
    bs = []
    for h in range(H):
        scores = mm(dm_s[:, head(h)], v_s[:, head(h)], 1, 1)
        bs.append(jnp.where(causal, scores, 0.0).astype(BF16))
        dqkv_s[0, :, head(h)] = (
            mm(bs[h], k_s[:, head(h)], 1, 0) + mm(dm_s[:, head(h)], carried_s[h], 1, 1)
        ).astype(BF16)
    gather_start(1, dqkv_s[0].astype(F32))
    chain(1)
    columns_start(1, nb_s[...].astype(F32))
    att_ref[...] = mm(nb_s[...], wo[...], 1, 0).astype(BF16)
    for h in range(H):
        mixed_s[:, head(h)] = mm(bs[h], q_s[:, head(h)], 0, 0)
        back_s[:, head(h)] = mm(attn_s[h], dm_s[:, head(h)], 0, 0)
    gather_forward(0)
    columns_finish(0)
    columns_finish(1)
    gather_finish(0)
    partial(0)
    chain_finish(1, later_s)
    for h in range(H):
        dqkv_s[1, :, head(h)] = (
            mixed_s[:, head(h)] + mm(v_s[:, head(h)], later_s[h], 1, 1)
        ).astype(BF16)
    gather_start(2, dqkv_s[1].astype(F32))
    for h in range(H):
        dqkv_s[2, :, head(h)] = (
            back_s[:, head(h)] + mm(k_s[:, head(h)], later_s[h], 1, 0)
        ).astype(BF16)
    gather_start(3, dqkv_s[2].astype(F32))

    gather_forward(1)
    gather_finish(1)
    partial(1)
    pass_on(0)
    dtok = mm(dqkv_s[0], wq[...], 1, 1)
    dtok = dtok + mm(dqkv_s[1], wk[...], 1, 1)
    dtok_ref[...] = (dtok + mm(dqkv_s[2], wv[...], 1, 1)).astype(BF16)
    gather_forward(2)
    gather_finish(2)
    partial(2)
    pass_on(1)
    gather_forward(3)
    gather_finish(3)
    partial(3)
    pass_on(2)
    pass_on(3)
    for k in range(4):
        finish(k)
    for cond, copy in pending:
        if cond is None:
            copy.wait_send()
        else:
            pl.when(cond)(copy.wait_send)
    for k in range(4):
        for zp in range(n_z):
            @pl.when(z != zp)
            def _():
                block_up(k, zp).wait_send()


def local(n_seq, m, tokens, w_query, w_key, w_value, w_output, out_cotangent):
    _, t_rows, width = tokens.shape
    dh = width // H
    n_z, members = n_seq // 2, 2 * m
    rows = width // (n_seq * m)
    vmem, dma = pltpu.VMEM, pltpu.SemaphoreType.DMA
    block = (t_rows, width)
    states = (2, H, dh, dh)
    in_vmem = pl.BlockSpec(memory_space=pltpu.VMEM)
    anywhere = pl.BlockSpec(memory_space=pl.ANY)
    attended, d_tokens, weight_grads = pl.pallas_call(
        functools.partial(kernel, n_seq, m),
        out_shape=(
            jax.ShapeDtypeStruct(block, BF16),
            jax.ShapeDtypeStruct(block, BF16),
            jax.ShapeDtypeStruct((rows, 4 * width), F32),
        ),
        in_specs=[in_vmem, in_vmem] + [anywhere] * 4,
        out_specs=(in_vmem,) * 3,
        scratch_shapes=[vmem((width, width), BF16)] * 4
        + [
            vmem(block, BF16),
            vmem(block, BF16),
            vmem(block, BF16),
            vmem((H, t_rows, t_rows), BF16),
            vmem(block, F32),
            vmem(block, F32),
            vmem((H, dh, dh), BF16),
            vmem((H, dh, dh), BF16),
            vmem(block, BF16),
            vmem(block, BF16),
            vmem((3,) + block, BF16),
            vmem((4, members) + block, F32),
            vmem((2, n_z, 2, m, rows, t_rows), F32),
            vmem((2, members, n_z, rows, t_rows), F32),
            vmem((2, n_z * rows, members * t_rows), BF16),
            vmem((4, n_z, rows, width), F32),
            vmem((4, n_z + 1, rows, width), F32),
            vmem(states, F32),
            vmem(states, F32),
            vmem(states, F32),
            vmem((2, H // 2, dh, dh), F32),
            dma((4,)),
            dma((4, m)),
            dma((4, m)),
            dma((4, members)),
            dma((2, members)),
            dma((2, members)),
            dma((2,)),
            dma((2,)),
            dma((2, H // 2)),
            dma((2, H // 2)),
            dma((2, H // 2)),
            dma((2, H // 2)),
            dma((4, n_z)),
            dma((4, n_z + 1)),
        ],
        compiler_params=pltpu.CompilerParams(
            collective_id=0, has_side_effects=True, vmem_limit_bytes=60 * 2**20
        ),
    )(
        tokens.reshape(block), out_cotangent.reshape(block),
        w_query, w_key, w_value, w_output,
    )
    return attended.reshape(tokens.shape), d_tokens.reshape(tokens.shape), weight_grads


def solution(mesh):
    batch = P(("groups", "dp"), "seq", None)
    return jax.shard_map(
        functools.partial(local, mesh.shape["seq"], mesh.shape["dp"]),
        mesh=mesh,
        in_specs=(batch, P(), P(), P(), P(), batch),
        out_specs=(batch, batch, P(("groups", "seq", "dp"), None)),
        check_vma=False,
    )
```

```python
import functools
import math

import jax
import jax.numpy as jnp
from jax import lax
from jax.experimental import pallas as pl
from jax.experimental.pallas import tpu as pltpu
from jax.sharding import PartitionSpec as P

H = 8
EPSILON = 1e-05
MESH = pl.DeviceIdType.MESH
F32, BF16 = jnp.float32, jnp.bfloat16
COLUMN_BLOCK = (3, 0, 1, 2)
SPLIT = 2


def mm(a, b, ca, cb):
    return lax.dot_general(a, b, (((ca,), (cb,)), ((), ())), preferred_element_type=F32)


def kernel(
    n_seq, m,
    tok_ref, cot_ref, wq_hbm, wk_hbm, wv_hbm, wo_hbm,
    att_ref, dtok_ref, wg_ref,
    wq, wk, wv, wo,
    q_s, k_s, v_s, attn_s, bs_s, mixed_s, back_s, carried_s, later_s, dm_s, nb_s, dqkv_s,
    gbuf, xt, xland, lhs, part, inb, sown, spart, crecv, csend,
    w_sem, g_send, g_fwd, g_recv, x_send, x_recv, e_send, e_recv,
    c_send, c_recv, p_send, p_recv, r_send, r_recv,
):
    t_rows, width = tok_ref.shape
    dh = width // H
    half = H // 2
    n_z = n_seq // 2
    rows = wg_ref.shape[0]
    members = 2 * m
    s, d = lax.axis_index("seq"), lax.axis_index("dp")
    z, c = lax.div(s, 2), lax.rem(s, 2)
    me = c * m + d
    up, down = z < n_z - 1, z > 0
    partner = {"seq": 2 * z + 1 - c, "dp": d}
    above = {"seq": jnp.minimum(s + 2, n_seq - 2 + c), "dp": d}
    below = {"seq": jnp.maximum(s - 2, c), "dp": d}
    part_width = width // SPLIT

    def rcopy(src, dst, ss, rs, dev):
        return pltpu.make_async_remote_copy(
            src_ref=src, dst_ref=dst, send_sem=ss, recv_sem=rs,
            device_id=dev, device_id_type=MESH,
        )

    def arrived(ref, sem):
        rcopy(ref, ref, w_sem.at[0], sem, partner).wait_recv()

    loads = [
        pltpu.make_async_copy(src, dst, w_sem.at[i])
        for i, (src, dst) in enumerate(
            ((wk_hbm, wk), (wv_hbm, wv), (wq_hbm, wq), (wo_hbm, wo))
        )
    ]
    for load in loads:
        load.start()

    def member(rel):
        t = lax.rem(me + rel, members)
        return t, lax.div(t, m), lax.rem(t, m)

    barrier = pltpu.get_barrier_semaphore()
    for rel in range(1, members):
        _, tc, td = member(rel)
        pl.semaphore_signal(
            barrier, inc=1, device_id={"seq": 2 * z + tc, "dp": td}, device_id_type=MESH
        )

    @pl.when(up)
    def _():
        pl.semaphore_signal(barrier, inc=1, device_id=above, device_id_type=MESH)

    @pl.when(down)
    def _():
        pl.semaphore_signal(barrier, inc=1, device_id=below, device_id_type=MESH)

    def gather_copies(k):
        own = gbuf.at[k, me]
        copies = [rcopy(own, own, g_send.at[k, 0], g_recv.at[k, me], partner)]
        for j in range(1, m):
            to = {"seq": s, "dp": lax.rem(d + j, m)}
            copies.append(rcopy(own, own, g_send.at[k, j], g_recv.at[k, me], to))
        return copies

    def forward_copies(k):
        copies = []
        for j in range(1, m):
            slot = c * m + lax.rem(d + m - j, m)
            ref = gbuf.at[k, slot]
            copies.append(rcopy(ref, ref, g_fwd.at[k, j], g_recv.at[k, slot], partner))
        return copies

    def gather_start(matrix, value):
        for i in range(SPLIT):
            k = matrix * SPLIT + i
            gbuf[k, me] = value[:, i * part_width:(i + 1) * part_width].astype(F32)
            for copy in reversed(gather_copies(k)):
                copy.start()

    def gather_finish(k):
        for copy in forward_copies(k):
            copy.wait_recv()
            copy.start()
        for j in range(m):
            slot = (1 - c) * m + j
            arrived(gbuf.at[k, slot], g_recv.at[k, slot])

    def column_copies(kind):
        copies = []
        for rel in range(1, members):
            t, tc, td = member(rel)
            copies.append(rcopy(
                xt.at[kind, :, tc, td], xland.at[kind, me], x_send.at[kind, rel],
                x_recv.at[kind, me], {"seq": 2 * z + tc, "dp": td},
            ))
        return copies

    def columns_start(kind, value):
        xt[kind] = value.T.reshape(n_z, 2, m, rows, t_rows)
        xland[kind, me] = xt[kind, :, c, d]
        for copy in column_copies(kind):
            copy.start()

    def columns_finish(kind):
        for rel in range(1, members):
            t, _, _ = member(rel)
            arrived(xland.at[kind, t], x_recv.at[kind, t])
        for j in range(members):
            lhs[kind, :, j * t_rows:(j + 1) * t_rows] = (
                xland[kind, j].reshape(n_z * rows, t_rows).astype(BF16)
            )

    def exchange_copy(way):
        return rcopy(sown.at[way], spart.at[way], e_send.at[way], e_recv.at[way], partner)

    def ends(way):
        return (down, up, above) if way == 0 else (up, down, below)

    def chain_copies(way, j):
        h = c * half + j
        ref = crecv.at[way, h]
        side = rcopy(ref, ref, p_send.at[way, j], p_recv.at[way, j], partner)
        ahead = rcopy(
            csend.at[way, j], ref, c_send.at[way, j], c_recv.at[way, j], ends(way)[2]
        )
        return h, side, ahead

    def chain(way):
        has_in, has_out, _ = ends(way)
        arrived(spart.at[way], e_recv.at[way])

        @pl.when(jnp.logical_not(has_in))
        def _():
            crecv[way] = jnp.zeros(crecv.shape[1:], F32)

        for j in range(half):
            h, side, ahead = chain_copies(way, j)

            @pl.when(has_in)
            def _():
                arrived(crecv.at[way, h], c_recv.at[way, j])

            @pl.when(has_out)
            def _():
                csend[way, j] = crecv[way, h] + (sown[way, h] + spart[way, h])
                ahead.start()

            @pl.when(has_in)
            def _():
                side.start()

    def chain_finish(way, out):
        has_in = ends(way)[0]
        for j in range(half):
            @pl.when(has_in)
            def _():
                arrived(crecv.at[way, (1 - c) * half + j], p_recv.at[way, j])

        takes = c == 1 - way
        for h in range(H):
            out[h] = jnp.where(
                takes, crecv[way, h] + spart[way, h], crecv[way, h]
            ).astype(BF16)

    def block_up(k, zp):
        ref = part.at[k, zp]
        return rcopy(ref, inb.at[k, zp], r_send.at[k, zp], r_recv.at[k, zp], above)

    def block_down(k, zp):
        slot = jnp.where(zp == z - 1, n_z, zp)
        return rcopy(
            part.at[k, zp], inb.at[k, slot], r_send.at[k, zp], r_recv.at[k, slot], below
        )

    def partial(k):
        right = gbuf[k].reshape(members * t_rows, part_width).astype(BF16)
        left = lhs[1 if k < SPLIT else 0]
        part[k] = mm(left, right, 1, 0).reshape(n_z, rows, part_width)

        @pl.when(z == 0)
        def _():
            for zp in reversed(range(1, n_z)):
                block_up(k, zp).start()

        @pl.when(z == n_z - 1)
        def _():
            for zp in range(n_z - 1):
                block_down(k, zp).start()

    def pass_on(k):
        for step in range(n_z - 1):
            high, low = n_z - 1 - step, step

            @pl.when((z > 0) & (z < high))
            def _():
                arrived(inb.at[k, high], r_recv.at[k, high])
                part[k, high] = part[k, high] + inb[k, high]
                block_up(k, high).start()

            @pl.when((z < n_z - 1) & (z > low))
            def _():
                arrived(inb.at[k, low], r_recv.at[k, low])
                part[k, low] = part[k, low] + inb[k, low]
                block_down(k, low).start()

    token_total = t_rows * n_seq * m

    def finish(k):
        @pl.when(down)
        def _():
            arrived(inb.at[k, z], r_recv.at[k, z])
            part[k, z] = part[k, z] + inb[k, z]

        @pl.when(up)
        def _():
            arrived(inb.at[k, n_z], r_recv.at[k, n_z])
            part[k, z] = part[k, z] + inb[k, n_z]

        at = COLUMN_BLOCK[k // SPLIT] * width + k % SPLIT * part_width
        wg_ref[:, at:at + part_width] = part[k, z] * (1.0 / math.sqrt(token_total))

    def head(h):
        return slice(h * dh, (h + 1) * dh)

    loads[0].wait()
    k_s[...] = mm(tok_ref[...], wk[...], 1, 0).astype(BF16)
    loads[1].wait()
    v_s[...] = mm(tok_ref[...], wv[...], 1, 0).astype(BF16)
    for h in range(H):
        sown[0, h] = mm(k_s[:, head(h)], v_s[:, head(h)], 0, 0)
    pl.semaphore_wait(
        barrier, members - 1 + jnp.where(up, 1, 0) + jnp.where(down, 1, 0)
    )
    exchange_copy(0).start()
    gather_start(0, cot_ref[...])
    loads[2].wait()
    q_s[...] = mm(tok_ref[...], wq[...], 1, 0).astype(BF16)
    first = z < n_z // 2
    last = jnp.logical_not(first)

    @pl.when(first)
    def _():
        chain(0)

    columns_start(0, tok_ref[...].astype(F32))
    loads[3].wait()
    back_s[...] = mm(cot_ref[...], wo[...], 1, 1)
    causal = lax.broadcasted_iota(jnp.int32, (t_rows, t_rows), 0) >= (
        lax.broadcasted_iota(jnp.int32, (t_rows, t_rows), 1)
    )
    for h in range(H):
        scores = mm(q_s[:, head(h)], k_s[:, head(h)], 1, 1)
        weights = jnp.where(causal, scores, 0.0).astype(BF16)
        attn_s[h] = weights
        mixed_s[:, head(h)] = mm(weights, v_s[:, head(h)], 1, 0)

    @pl.when(last)
    def _():
        chain(0)

    chain_finish(0, carried_s)
    for h in range(H):
        mixed_s[:, head(h)] += mm(q_s[:, head(h)], carried_s[h], 1, 0)

    mixed = mixed_s[...]
    scale_rows = jnp.sqrt(jnp.mean(mixed * mixed, axis=-1, keepdims=True) + EPSILON)
    normed = mixed / scale_rows
    nb_s[...] = normed.astype(BF16)
    back = back_s[...]
    dm_s[...] = (
        (back - normed * jnp.mean(back * normed, axis=-1, keepdims=True)) / scale_rows
    ).astype(BF16)
    for h in range(H):
        sown[1, h] = mm(q_s[:, head(h)], dm_s[:, head(h)], 0, 0)
    exchange_copy(1).start()
    columns_start(1, nb_s[...].astype(F32))

    @pl.when(last)
    def _():
        chain(1)

    for h in range(H):
        scores = mm(dm_s[:, head(h)], v_s[:, head(h)], 1, 1)
        bs_s[h] = jnp.where(causal, scores, 0.0).astype(BF16)
        dqkv_s[0, :, head(h)] = (
            mm(bs_s[h], k_s[:, head(h)], 1, 0) + mm(dm_s[:, head(h)], carried_s[h], 1, 1)
        ).astype(BF16)
    gather_start(1, dqkv_s[0])
    for h in range(H):
        mixed_s[:, head(h)] = mm(bs_s[h], q_s[:, head(h)], 0, 0)
        back_s[:, head(h)] = mm(attn_s[h], dm_s[:, head(h)], 0, 0)

    def chunks(matrix):
        return range(matrix * SPLIT, (matrix + 1) * SPLIT)

    def output_chunks():
        columns_finish(0)
        columns_finish(1)
        for k in chunks(0):
            gather_finish(k)
            partial(k)

    def query_chunks():
        for k in chunks(1):
            gather_finish(k)
            partial(k)

    @pl.when((z == 0) | last)
    def _():
        output_chunks()

    @pl.when(z == 0)
    def _():
        query_chunks()

    @pl.when(first)
    def _():
        chain(1)

    chain_finish(1, later_s)
    for h in range(H):
        dqkv_s[1, :, head(h)] = (
            mixed_s[:, head(h)] + mm(v_s[:, head(h)], later_s[h], 1, 1)
        ).astype(BF16)
    gather_start(2, dqkv_s[1])
    for h in range(H):
        dqkv_s[2, :, head(h)] = (
            back_s[:, head(h)] + mm(k_s[:, head(h)], later_s[h], 1, 0)
        ).astype(BF16)
    gather_start(3, dqkv_s[2])

    @pl.when((z > 0) & first)
    def _():
        output_chunks()

    @pl.when(z > 0)
    def _():
        query_chunks()

    for k in chunks(0):
        pass_on(k)
    att_ref[...] = mm(nb_s[...], wo[...], 1, 0).astype(BF16)
    dtok = mm(dqkv_s[0], wq[...], 1, 1)
    dtok = dtok + mm(dqkv_s[1], wk[...], 1, 1)
    dtok_ref[...] = (dtok + mm(dqkv_s[2], wv[...], 1, 1)).astype(BF16)
    count = 4 * SPLIT
    for k in range(2 * SPLIT, count):
        gather_finish(k)
        partial(k)
        pass_on(k - SPLIT)
        finish(k - 2 * SPLIT)
    for k in range(count - SPLIT, count):
        pass_on(k)
        finish(k - SPLIT)
    for k in range(count - SPLIT, count):
        finish(k)

    for way in range(2):
        exchange_copy(way).wait_send()
        for copy in column_copies(way):
            copy.wait_send()
        has_in, has_out, _ = ends(way)
        for j in range(half):
            _, side, ahead = chain_copies(way, j)
            pl.when(has_in)(side.wait_send)
            pl.when(has_out)(ahead.wait_send)
    for k in range(count):
        for copy in gather_copies(k) + forward_copies(k):
            copy.wait_send()
        for zp in range(n_z):
            @pl.when(z != zp)
            def _():
                block_up(k, zp).wait_send()


def copy_kernel(count, *refs):
    sems = refs[-1]
    copies = [
        pltpu.make_async_copy(refs[i], refs[count + i], sems.at[i]) for i in range(count)
    ]
    for copy in copies:
        copy.start()
    for copy in copies:
        copy.wait()


def copied(arrays):
    count = len(arrays)
    anywhere = pl.BlockSpec(memory_space=pl.ANY)
    return pl.pallas_call(
        functools.partial(copy_kernel, count),
        out_shape=tuple(jax.ShapeDtypeStruct(a.shape, a.dtype) for a in arrays),
        in_specs=[anywhere] * count,
        out_specs=(anywhere,) * count,
        scratch_shapes=[pltpu.SemaphoreType.DMA((count,))],
    )(*arrays)


def local(n_seq, m, tokens, w_query, w_key, w_value, w_output, out_cotangent):
    _, t_rows, width = tokens.shape
    dh = width // H
    n_z, members = n_seq // 2, 2 * m
    rows = width // (n_seq * m)
    count = 4 * SPLIT
    vmem, dma = pltpu.VMEM, pltpu.SemaphoreType.DMA
    block = (t_rows, width)
    states = (2, H, dh, dh)
    in_vmem = pl.BlockSpec(memory_space=pltpu.VMEM)
    anywhere = pl.BlockSpec(memory_space=pl.ANY)
    results = pl.pallas_call(
        functools.partial(kernel, n_seq, m),
        out_shape=(
            jax.ShapeDtypeStruct(block, BF16),
            jax.ShapeDtypeStruct(block, BF16),
            jax.ShapeDtypeStruct((rows, 4 * width), F32),
        ),
        in_specs=[in_vmem, in_vmem] + [anywhere] * 4,
        out_specs=(in_vmem,) * 3,
        scratch_shapes=[vmem((width, width), BF16)] * 4
        + [
            vmem(block, BF16),
            vmem(block, BF16),
            vmem(block, BF16),
            vmem((H, t_rows, t_rows), BF16),
            vmem((H, t_rows, t_rows), BF16),
            vmem(block, F32),
            vmem(block, F32),
            vmem((H, dh, dh), BF16),
            vmem((H, dh, dh), BF16),
            vmem(block, BF16),
            vmem(block, BF16),
            vmem((3,) + block, BF16),
            vmem((count, members, t_rows, width // SPLIT), F32),
            vmem((2, n_z, 2, m, rows, t_rows), F32),
            vmem((2, members, n_z, rows, t_rows), F32),
            vmem((2, n_z * rows, members * t_rows), BF16),
            vmem((count, n_z, rows, width // SPLIT), F32),
            vmem((count, n_z + 1, rows, width // SPLIT), F32),
            vmem(states, F32),
            vmem(states, F32),
            vmem(states, F32),
            vmem((2, H // 2, dh, dh), F32),
            dma((4,)),
            dma((count, m)),
            dma((count, m)),
            dma((count, members)),
            dma((2, members)),
            dma((2, members)),
            dma((2,)),
            dma((2,)),
            dma((2, H // 2)),
            dma((2, H // 2)),
            dma((2, H // 2)),
            dma((2, H // 2)),
            dma((count, n_z)),
            dma((count, n_z + 1)),
        ],
        compiler_params=pltpu.CompilerParams(
            collective_id=0, has_side_effects=True, vmem_limit_bytes=60 * 2**20
        ),
    )(
        tokens.reshape(block), out_cotangent.reshape(block),
        w_query, w_key, w_value, w_output,
    )
    attended, d_tokens, weight_grads = copied(results)
    return attended.reshape(tokens.shape), d_tokens.reshape(tokens.shape), weight_grads


def solution(mesh):
    batch = P(("groups", "dp"), "seq", None)
    return jax.shard_map(
        functools.partial(local, mesh.shape["seq"], mesh.shape["dp"]),
        mesh=mesh,
        in_specs=(batch, P(), P(), P(), P(), batch),
        out_specs=(batch, batch, P(("groups", "seq", "dp"), None)),
        check_vma=False,
    )
```

```python
import functools
import math

import jax
import jax.numpy as jnp
from jax import lax
from jax.experimental import pallas as pl
from jax.experimental.pallas import tpu as pltpu
from jax.sharding import PartitionSpec as P

H = 8
EPSILON = 1e-05
MESH = pl.DeviceIdType.MESH
F32, BF16 = jnp.float32, jnp.bfloat16
COLUMN_BLOCK = (3, 0, 1, 2)
SPLIT = 1


def mm(a, b, ca, cb):
    return lax.dot_general(a, b, (((ca,), (cb,)), ((), ())), preferred_element_type=F32)


def kernel(
    n_seq, m,
    tok_ref, cot_ref, wq_hbm, wk_hbm, wv_hbm, wo_hbm,
    att_ref, dtok_ref, wg_ref,
    wq, wk, wv, wo,
    q_s, k_s, v_s, attn_s, bs_s, mixed_s, back_s, carried_s, later_s, dm_s, nb_s, dqkv_s,
    gbuf, xt, xland, lhs, part, inb, sown, spart, crecv, csend,
    w_sem, g_send, g_fwd, g_recv, x_send, x_recv, e_send, e_recv,
    c_send, c_recv, p_send, p_recv, r_send, r_recv,
):
    t_rows, width = tok_ref.shape
    dh = width // H
    half = H // 2
    n_z = n_seq // 2
    rows = wg_ref.shape[0]
    members = 2 * m
    s, d = lax.axis_index("seq"), lax.axis_index("dp")
    z, c = lax.div(s, 2), lax.rem(s, 2)
    me = c * m + d
    up, down = z < n_z - 1, z > 0
    partner = {"seq": 2 * z + 1 - c, "dp": d}
    above = {"seq": jnp.minimum(s + 2, n_seq - 2 + c), "dp": d}
    below = {"seq": jnp.maximum(s - 2, c), "dp": d}
    part_width = width // SPLIT

    def rcopy(src, dst, ss, rs, dev):
        return pltpu.make_async_remote_copy(
            src_ref=src, dst_ref=dst, send_sem=ss, recv_sem=rs,
            device_id=dev, device_id_type=MESH,
        )

    def arrived(ref, sem):
        rcopy(ref, ref, w_sem.at[0], sem, partner).wait_recv()

    loads = [
        pltpu.make_async_copy(src, dst, w_sem.at[i])
        for i, (src, dst) in enumerate(
            ((wk_hbm, wk), (wv_hbm, wv), (wq_hbm, wq), (wo_hbm, wo))
        )
    ]
    for load in loads:
        load.start()

    def member(rel):
        t = lax.rem(me + rel, members)
        return t, lax.div(t, m), lax.rem(t, m)

    barrier = pltpu.get_barrier_semaphore()
    for rel in range(1, members):
        _, tc, td = member(rel)
        pl.semaphore_signal(
            barrier, inc=1, device_id={"seq": 2 * z + tc, "dp": td}, device_id_type=MESH
        )

    @pl.when(up)
    def _():
        pl.semaphore_signal(barrier, inc=1, device_id=above, device_id_type=MESH)

    @pl.when(down)
    def _():
        pl.semaphore_signal(barrier, inc=1, device_id=below, device_id_type=MESH)

    def gather_copies(k):
        own = gbuf.at[k, me]
        copies = [rcopy(own, own, g_send.at[k, 0], g_recv.at[k, me], partner)]
        for j in range(1, m):
            to = {"seq": s, "dp": lax.rem(d + j, m)}
            copies.append(rcopy(own, own, g_send.at[k, j], g_recv.at[k, me], to))
        return copies

    def forward_copies(k):
        copies = []
        for j in range(1, m):
            slot = c * m + lax.rem(d + m - j, m)
            ref = gbuf.at[k, slot]
            copies.append(rcopy(ref, ref, g_fwd.at[k, j], g_recv.at[k, slot], partner))
        return copies

    def gather_start(matrix, value):
        for i in range(SPLIT):
            k = matrix * SPLIT + i
            gbuf[k, me] = value[:, i * part_width:(i + 1) * part_width].astype(F32)
            for copy in reversed(gather_copies(k)):
                copy.start()

    def gather_finish(k):
        for copy in forward_copies(k):
            copy.wait_recv()
            copy.start()
        for j in range(m):
            slot = (1 - c) * m + j
            arrived(gbuf.at[k, slot], g_recv.at[k, slot])

    def column_copies(kind):
        copies = []
        for rel in range(1, members):
            t, tc, td = member(rel)
            copies.append(rcopy(
                xt.at[kind, :, tc, td], xland.at[kind, me], x_send.at[kind, rel],
                x_recv.at[kind, me], {"seq": 2 * z + tc, "dp": td},
            ))
        return copies

    def columns_start(kind, value):
        xt[kind] = value.T.reshape(n_z, 2, m, rows, t_rows)
        xland[kind, me] = xt[kind, :, c, d]
        for copy in column_copies(kind):
            copy.start()

    def columns_finish(kind):
        for rel in range(1, members):
            t, _, _ = member(rel)
            arrived(xland.at[kind, t], x_recv.at[kind, t])
        for j in range(members):
            lhs[kind, :, j * t_rows:(j + 1) * t_rows] = (
                xland[kind, j].reshape(n_z * rows, t_rows).astype(BF16)
            )

    def exchange_copy(way):
        return rcopy(sown.at[way], spart.at[way], e_send.at[way], e_recv.at[way], partner)

    def ends(way):
        return (down, up, above) if way == 0 else (up, down, below)

    def chain_copies(way, j):
        h = c * half + j
        ref = crecv.at[way, h]
        side = rcopy(ref, ref, p_send.at[way, j], p_recv.at[way, j], partner)
        ahead = rcopy(
            csend.at[way, j], ref, c_send.at[way, j], c_recv.at[way, j], ends(way)[2]
        )
        return h, side, ahead

    def chain(way):
        has_in, has_out, _ = ends(way)
        arrived(spart.at[way], e_recv.at[way])

        @pl.when(jnp.logical_not(has_in))
        def _():
            crecv[way] = jnp.zeros(crecv.shape[1:], F32)

        for j in range(half):
            h, side, ahead = chain_copies(way, j)

            @pl.when(has_in)
            def _():
                arrived(crecv.at[way, h], c_recv.at[way, j])

            @pl.when(has_out)
            def _():
                csend[way, j] = crecv[way, h] + (sown[way, h] + spart[way, h])
                ahead.start()

            @pl.when(has_in)
            def _():
                side.start()

    def chain_finish(way, out):
        has_in = ends(way)[0]
        for j in range(half):
            @pl.when(has_in)
            def _():
                arrived(crecv.at[way, (1 - c) * half + j], p_recv.at[way, j])

        takes = c == 1 - way
        for h in range(H):
            out[h] = jnp.where(
                takes, crecv[way, h] + spart[way, h], crecv[way, h]
            ).astype(BF16)

    def block_up(k, zp):
        ref = part.at[k, zp]
        return rcopy(ref, inb.at[k, zp], r_send.at[k, zp], r_recv.at[k, zp], above)

    def block_down(k, zp):
        slot = jnp.where(zp == z - 1, n_z, zp)
        return rcopy(
            part.at[k, zp], inb.at[k, slot], r_send.at[k, zp], r_recv.at[k, slot], below
        )

    def partial(k):
        right = gbuf[k].reshape(members * t_rows, part_width).astype(BF16)
        left = lhs[1 if k < SPLIT else 0]
        part[k] = mm(left, right, 1, 0).reshape(n_z, rows, part_width)

        @pl.when(z == 0)
        def _():
            for zp in reversed(range(1, n_z)):
                block_up(k, zp).start()

        @pl.when(z == n_z - 1)
        def _():
            for zp in range(n_z - 1):
                block_down(k, zp).start()

    def pass_on(k):
        for step in range(n_z - 1):
            high, low = n_z - 1 - step, step

            @pl.when((z > 0) & (z < high))
            def _():
                arrived(inb.at[k, high], r_recv.at[k, high])
                part[k, high] = part[k, high] + inb[k, high]
                block_up(k, high).start()

            @pl.when((z < n_z - 1) & (z > low))
            def _():
                arrived(inb.at[k, low], r_recv.at[k, low])
                part[k, low] = part[k, low] + inb[k, low]
                block_down(k, low).start()

    token_total = t_rows * n_seq * m

    def finish(k):
        @pl.when(down)
        def _():
            arrived(inb.at[k, z], r_recv.at[k, z])
            part[k, z] = part[k, z] + inb[k, z]

        @pl.when(up)
        def _():
            arrived(inb.at[k, n_z], r_recv.at[k, n_z])
            part[k, z] = part[k, z] + inb[k, n_z]

        at = COLUMN_BLOCK[k // SPLIT] * width + k % SPLIT * part_width
        wg_ref[:, at:at + part_width] = part[k, z] * (1.0 / math.sqrt(token_total))

    def head(h):
        return slice(h * dh, (h + 1) * dh)

    loads[0].wait()
    k_s[...] = mm(tok_ref[...], wk[...], 1, 0).astype(BF16)
    loads[1].wait()
    v_s[...] = mm(tok_ref[...], wv[...], 1, 0).astype(BF16)
    for h in range(H):
        sown[0, h] = mm(k_s[:, head(h)], v_s[:, head(h)], 0, 0)
    pl.semaphore_wait(
        barrier, members - 1 + jnp.where(up, 1, 0) + jnp.where(down, 1, 0)
    )
    exchange_copy(0).start()
    gather_start(0, cot_ref[...])
    loads[2].wait()
    q_s[...] = mm(tok_ref[...], wq[...], 1, 0).astype(BF16)
    lowest, highest = z == 0, z == n_z - 1
    middle = (z > 0) & (z < n_z - 1)

    @pl.when(lowest)
    def _():
        chain(0)

    columns_start(0, tok_ref[...].astype(F32))
    loads[3].wait()
    back_s[...] = mm(cot_ref[...], wo[...], 1, 1)

    @pl.when(middle)
    def _():
        chain(0)

    causal = lax.broadcasted_iota(jnp.int32, (t_rows, t_rows), 0) >= (
        lax.broadcasted_iota(jnp.int32, (t_rows, t_rows), 1)
    )
    for h in range(H):
        scores = mm(q_s[:, head(h)], k_s[:, head(h)], 1, 1)
        weights = jnp.where(causal, scores, 0.0).astype(BF16)
        attn_s[h] = weights
        mixed_s[:, head(h)] = mm(weights, v_s[:, head(h)], 1, 0)

    @pl.when(highest)
    def _():
        chain(0)

    chain_finish(0, carried_s)
    for h in range(H):
        mixed_s[:, head(h)] += mm(q_s[:, head(h)], carried_s[h], 1, 0)

    mixed = mixed_s[...]
    scale_rows = jnp.sqrt(jnp.mean(mixed * mixed, axis=-1, keepdims=True) + EPSILON)
    normed = mixed / scale_rows
    nb_s[...] = normed.astype(BF16)
    back = back_s[...]
    dm_s[...] = (
        (back - normed * jnp.mean(back * normed, axis=-1, keepdims=True)) / scale_rows
    ).astype(BF16)
    for h in range(H):
        sown[1, h] = mm(q_s[:, head(h)], dm_s[:, head(h)], 0, 0)
    exchange_copy(1).start()
    columns_start(1, nb_s[...].astype(F32))

    @pl.when(highest)
    def _():
        chain(1)

    for h in range(H):
        scores = mm(dm_s[:, head(h)], v_s[:, head(h)], 1, 1)
        bs_s[h] = jnp.where(causal, scores, 0.0).astype(BF16)
        dqkv_s[0, :, head(h)] = (
            mm(bs_s[h], k_s[:, head(h)], 1, 0) + mm(dm_s[:, head(h)], carried_s[h], 1, 1)
        ).astype(BF16)
    gather_start(1, dqkv_s[0])

    @pl.when(middle)
    def _():
        chain(1)

    for h in range(H):
        mixed_s[:, head(h)] = mm(bs_s[h], q_s[:, head(h)], 0, 0)
        back_s[:, head(h)] = mm(attn_s[h], dm_s[:, head(h)], 0, 0)

    def chunks(matrix):
        return range(matrix * SPLIT, (matrix + 1) * SPLIT)

    def output_chunks():
        columns_finish(0)
        columns_finish(1)
        for k in chunks(0):
            gather_finish(k)
            partial(k)

    def query_chunks():
        for k in chunks(1):
            gather_finish(k)
            partial(k)

    output_chunks()

    @pl.when(lowest)
    def _():
        query_chunks()
        chain(1)

    chain_finish(1, later_s)
    for h in range(H):
        dqkv_s[1, :, head(h)] = (
            mixed_s[:, head(h)] + mm(v_s[:, head(h)], later_s[h], 1, 1)
        ).astype(BF16)
    gather_start(2, dqkv_s[1])
    for h in range(H):
        dqkv_s[2, :, head(h)] = (
            back_s[:, head(h)] + mm(k_s[:, head(h)], later_s[h], 1, 0)
        ).astype(BF16)
    gather_start(3, dqkv_s[2])

    @pl.when(z > 0)
    def _():
        query_chunks()

    for k in chunks(0):
        pass_on(k)
    att_ref[...] = mm(nb_s[...], wo[...], 1, 0).astype(BF16)
    dtok = mm(dqkv_s[0], wq[...], 1, 1)
    dtok = dtok + mm(dqkv_s[1], wk[...], 1, 1)
    dtok_ref[...] = (dtok + mm(dqkv_s[2], wv[...], 1, 1)).astype(BF16)
    count = 4 * SPLIT
    for k in range(2 * SPLIT, count):
        gather_finish(k)
        partial(k)
        pass_on(k - SPLIT)
        finish(k - 2 * SPLIT)
    for k in range(count - SPLIT, count):
        pass_on(k)
        finish(k - SPLIT)
    for k in range(count - SPLIT, count):
        finish(k)

    for way in range(2):
        exchange_copy(way).wait_send()
        for copy in column_copies(way):
            copy.wait_send()
        has_in, has_out, _ = ends(way)
        for j in range(half):
            _, side, ahead = chain_copies(way, j)
            pl.when(has_in)(side.wait_send)
            pl.when(has_out)(ahead.wait_send)
    for k in range(count):
        for copy in gather_copies(k) + forward_copies(k):
            copy.wait_send()
        for zp in range(n_z):
            @pl.when(z != zp)
            def _():
                block_up(k, zp).wait_send()


def copy_kernel(count, *refs):
    sources, results, held = refs[:count], refs[count:2 * count], refs[2 * count:3 * count]
    sems = refs[-1]
    loads = [
        pltpu.make_async_copy(sources[i], held[i], sems.at[0, i]) for i in range(count)
    ]
    stores = [
        pltpu.make_async_copy(held[i], results[i], sems.at[1, i]) for i in range(count)
    ]
    for load in loads:
        load.start()
    for load, store in zip(loads, stores):
        load.wait()
        store.start()
    for store in stores:
        store.wait()


def copied(arrays):
    count = len(arrays)
    anywhere = pl.BlockSpec(memory_space=pl.ANY)
    return pl.pallas_call(
        functools.partial(copy_kernel, count),
        out_shape=tuple(jax.ShapeDtypeStruct(a.shape, a.dtype) for a in arrays),
        in_specs=[anywhere] * count,
        out_specs=(anywhere,) * count,
        scratch_shapes=[pltpu.VMEM(a.shape, a.dtype) for a in arrays]
        + [pltpu.SemaphoreType.DMA((2, count))],
    )(*arrays)


def local(n_seq, m, tokens, w_query, w_key, w_value, w_output, out_cotangent):
    _, t_rows, width = tokens.shape
    dh = width // H
    n_z, members = n_seq // 2, 2 * m
    rows = width // (n_seq * m)
    count = 4 * SPLIT
    vmem, dma = pltpu.VMEM, pltpu.SemaphoreType.DMA
    block = (t_rows, width)
    states = (2, H, dh, dh)
    in_vmem = pl.BlockSpec(memory_space=pltpu.VMEM)
    anywhere = pl.BlockSpec(memory_space=pl.ANY)
    results = pl.pallas_call(
        functools.partial(kernel, n_seq, m),
        out_shape=(
            jax.ShapeDtypeStruct(block, BF16),
            jax.ShapeDtypeStruct(block, BF16),
            jax.ShapeDtypeStruct((rows, 4 * width), F32),
        ),
        in_specs=[in_vmem, in_vmem] + [anywhere] * 4,
        out_specs=(in_vmem,) * 3,
        scratch_shapes=[vmem((width, width), BF16)] * 4
        + [
            vmem(block, BF16),
            vmem(block, BF16),
            vmem(block, BF16),
            vmem((H, t_rows, t_rows), BF16),
            vmem((H, t_rows, t_rows), BF16),
            vmem(block, F32),
            vmem(block, F32),
            vmem((H, dh, dh), BF16),
            vmem((H, dh, dh), BF16),
            vmem(block, BF16),
            vmem(block, BF16),
            vmem((3,) + block, BF16),
            vmem((count, members, t_rows, width // SPLIT), F32),
            vmem((2, n_z, 2, m, rows, t_rows), F32),
            vmem((2, members, n_z, rows, t_rows), F32),
            vmem((2, n_z * rows, members * t_rows), BF16),
            vmem((count, n_z, rows, width // SPLIT), F32),
            vmem((count, n_z + 1, rows, width // SPLIT), F32),
            vmem(states, F32),
            vmem(states, F32),
            vmem(states, F32),
            vmem((2, H // 2, dh, dh), F32),
            dma((4,)),
            dma((count, m)),
            dma((count, m)),
            dma((count, members)),
            dma((2, members)),
            dma((2, members)),
            dma((2,)),
            dma((2,)),
            dma((2, H // 2)),
            dma((2, H // 2)),
            dma((2, H // 2)),
            dma((2, H // 2)),
            dma((count, n_z)),
            dma((count, n_z + 1)),
        ],
        compiler_params=pltpu.CompilerParams(
            collective_id=0, has_side_effects=True, vmem_limit_bytes=60 * 2**20
        ),
    )(
        tokens.reshape(block), out_cotangent.reshape(block),
        w_query, w_key, w_value, w_output,
    )
    attended, d_tokens, weight_grads = copied(results)
    return attended.reshape(tokens.shape), d_tokens.reshape(tokens.shape), weight_grads


def solution(mesh):
    batch = P(("groups", "dp"), "seq", None)
    return jax.shard_map(
        functools.partial(local, mesh.shape["seq"], mesh.shape["dp"]),
        mesh=mesh,
        in_specs=(batch, P(), P(), P(), P(), batch),
        out_specs=(batch, batch, P(("groups", "seq", "dp"), None)),
        check_vma=False,
    )
```

```python
import functools
import math

import jax
import jax.numpy as jnp
from jax import lax
from jax.experimental import pallas as pl
from jax.experimental.pallas import tpu as pltpu
from jax.sharding import PartitionSpec as P

H = 8
EPSILON = 1e-05
MESH = pl.DeviceIdType.MESH
F32, BF16 = jnp.float32, jnp.bfloat16
COLUMN_BLOCK = (3, 0, 1, 2)
SPLIT = 1


def leads(members):
    return members <= 8


def mm(a, b, ca, cb):
    return lax.dot_general(a, b, (((ca,), (cb,)), ((), ())), preferred_element_type=F32)


def kernel(
    n_seq, m,
    tok_ref, cot_ref, wq_hbm, wk_hbm, wv_hbm, wo_hbm,
    att_ref, dtok_ref, wg_ref,
    wq, wk, wv, wo,
    q_s, k_s, v_s, attn_s, bs_s, mixed_s, back_s, carried_s, later_s, dm_s, nb_s, dqkv_s,
    gbuf, xt, xland, lhs, part, inb, sown, spart, crecv, csend,
    w_sem, g_send, g_fwd, g_recv, x_send, x_recv, e_send, e_recv,
    c_send, c_recv, p_send, p_recv, r_send, r_recv,
    top_g, top_x, top_lhs, t_send, t_out, t_fwd, t_recv, tx_send, tx_recv,
):
    t_rows, width = tok_ref.shape
    dh = width // H
    half = H // 2
    n_z = n_seq // 2
    rows = wg_ref.shape[0]
    members = 2 * m
    s, d = lax.axis_index("seq"), lax.axis_index("dp")
    z, c = lax.div(s, 2), lax.rem(s, 2)
    me = c * m + d
    up, down = z < n_z - 1, z > 0
    lead = leads(members)
    top, under = (z == n_z - 1) & lead, (z == n_z - 2) & lead
    partner = {"seq": 2 * z + 1 - c, "dp": d}
    above = {"seq": jnp.minimum(s + 2, n_seq - 2 + c), "dp": d}
    below = {"seq": jnp.maximum(s - 2, c), "dp": d}
    part_width = width // SPLIT

    def rcopy(src, dst, ss, rs, dev):
        return pltpu.make_async_remote_copy(
            src_ref=src, dst_ref=dst, send_sem=ss, recv_sem=rs,
            device_id=dev, device_id_type=MESH,
        )

    def arrived(ref, sem):
        rcopy(ref, ref, w_sem.at[0], sem, partner).wait_recv()

    loads = [
        pltpu.make_async_copy(src, dst, w_sem.at[i])
        for i, (src, dst) in enumerate(
            ((wk_hbm, wk), (wv_hbm, wv), (wq_hbm, wq), (wo_hbm, wo))
        )
    ]
    for load in loads:
        load.start()

    def member(rel):
        t = lax.rem(me + rel, members)
        return t, lax.div(t, m), lax.rem(t, m)

    barrier = pltpu.get_barrier_semaphore()
    for rel in range(1, members):
        _, tc, td = member(rel)
        pl.semaphore_signal(
            barrier, inc=1, device_id={"seq": 2 * z + tc, "dp": td}, device_id_type=MESH
        )

    @pl.when(up & jnp.logical_not(under))
    def _():
        pl.semaphore_signal(barrier, inc=1, device_id=above, device_id_type=MESH)

    @pl.when(under)
    def _():
        for t in range(members):
            pl.semaphore_signal(
                barrier, inc=1, device_id={"seq": 2 * (z + 1) + t // m, "dp": t % m},
                device_id_type=MESH,
            )

    @pl.when(down)
    def _():
        pl.semaphore_signal(barrier, inc=1, device_id=below, device_id_type=MESH)

    def gather_copies(k):
        own = gbuf.at[k, me]
        copies = [rcopy(own, own, g_send.at[k, 0], g_recv.at[k, me], partner)]
        for j in range(1, m):
            to = {"seq": s, "dp": lax.rem(d + j, m)}
            copies.append(rcopy(own, own, g_send.at[k, j], g_recv.at[k, me], to))
        return copies

    def forward_copies(k):
        copies = []
        for j in range(1, m):
            slot = c * m + lax.rem(d + m - j, m)
            ref = gbuf.at[k, slot]
            copies.append(rcopy(ref, ref, g_fwd.at[k, j], g_recv.at[k, slot], partner))
        return copies

    def gather_start(matrix, value):
        for i in range(SPLIT):
            k = matrix * SPLIT + i
            gbuf[k, me] = value[:, i * part_width:(i + 1) * part_width].astype(F32)
            for copy in reversed(gather_copies(k)):
                copy.start()

    def gather_finish(k):
        for copy in forward_copies(k):
            copy.wait_recv()
            copy.start()
        for j in range(m):
            slot = (1 - c) * m + j
            arrived(gbuf.at[k, slot], g_recv.at[k, slot])

    def column_copies(kind):
        copies = []
        for rel in range(1, members):
            t, tc, td = member(rel)
            copies.append(rcopy(
                xt.at[kind, :, tc, td], xland.at[kind, me], x_send.at[kind, rel],
                x_recv.at[kind, me], {"seq": 2 * z + tc, "dp": td},
            ))
        return copies

    def columns_start(kind, value):
        xt[kind] = value.T.reshape(n_z, 2, m, rows, t_rows)
        xland[kind, me] = xt[kind, :, c, d]
        for copy in column_copies(kind):
            copy.start()

    def columns_finish(kind):
        for rel in range(1, members):
            t, _, _ = member(rel)
            arrived(xland.at[kind, t], x_recv.at[kind, t])
        for j in range(members):
            lhs[kind, :, j * t_rows:(j + 1) * t_rows] = (
                xland[kind, j].reshape(n_z * rows, t_rows).astype(BF16)
            )

    def top_copies():
        return [
            rcopy(gbuf.at[i, me], top_g.at[i, me], t_send.at[i], t_recv.at[i, me], below)
            for i in range(SPLIT)
        ]

    def top_gather_copies(i):
        own = top_g.at[i, me]
        copies = [rcopy(own, own, t_out.at[i, 0], t_recv.at[i, me], partner)]
        for j in range(1, m):
            to = {"seq": s, "dp": lax.rem(d + j, m)}
            copies.append(rcopy(own, own, t_out.at[i, j], t_recv.at[i, me], to))
        return copies

    def top_forward_copies(i):
        copies = []
        for j in range(1, m):
            slot = c * m + lax.rem(d + m - j, m)
            ref = top_g.at[i, slot]
            copies.append(rcopy(ref, ref, t_fwd.at[i, j], t_recv.at[i, slot], partner))
        return copies

    def top_column_copies():
        return [
            rcopy(
                xt.at[1, pl.ds(0, n_z - 1), t // m, t % m], top_x.at[me], tx_send.at[t],
                tx_recv.at[me], {"seq": jnp.maximum(2 * (z - 1), 0) + t // m, "dp": t % m},
            )
            for t in range(members)
        ]

    def top_finish():
        for t in range(members):
            arrived(top_x.at[t], tx_recv.at[t])
            top_lhs[:, t * t_rows:(t + 1) * t_rows] = (
                top_x[t].reshape((n_z - 1) * rows, t_rows).astype(BF16)
            )
        for i in range(SPLIT):
            for copy in top_forward_copies(i):
                copy.wait_recv()
                copy.start()
            for j in range(m):
                slot = (1 - c) * m + j
                arrived(top_g.at[i, slot], t_recv.at[i, slot])

    def highest_of(k):
        return n_z - 2 if lead and k < SPLIT else n_z - 1

    def exchange_copy(way):
        return rcopy(sown.at[way], spart.at[way], e_send.at[way], e_recv.at[way], partner)

    def ends(way):
        return (down, up, above) if way == 0 else (up, down, below)

    def chain_copies(way, j):
        h = c * half + j
        ref = crecv.at[way, h]
        side = rcopy(ref, ref, p_send.at[way, j], p_recv.at[way, j], partner)
        ahead = rcopy(
            csend.at[way, j], ref, c_send.at[way, j], c_recv.at[way, j], ends(way)[2]
        )
        return h, side, ahead

    def chain(way):
        has_in, has_out, _ = ends(way)
        arrived(spart.at[way], e_recv.at[way])

        @pl.when(jnp.logical_not(has_in))
        def _():
            crecv[way] = jnp.zeros(crecv.shape[1:], F32)

        for j in range(half):
            h, side, ahead = chain_copies(way, j)

            @pl.when(has_in)
            def _():
                arrived(crecv.at[way, h], c_recv.at[way, j])

            @pl.when(has_out)
            def _():
                csend[way, j] = crecv[way, h] + (sown[way, h] + spart[way, h])
                ahead.start()

            @pl.when(has_in)
            def _():
                side.start()

    def chain_finish(way, out):
        has_in = ends(way)[0]
        for j in range(half):
            @pl.when(has_in)
            def _():
                arrived(crecv.at[way, (1 - c) * half + j], p_recv.at[way, j])

        takes = c == 1 - way
        for h in range(H):
            out[h] = jnp.where(
                takes, crecv[way, h] + spart[way, h], crecv[way, h]
            ).astype(BF16)

    def block_up(k, zp):
        ref = part.at[k, zp]
        return rcopy(ref, inb.at[k, zp], r_send.at[k, zp], r_recv.at[k, zp], above)

    def block_down(k, zp):
        slot = jnp.where(zp == z - 1, n_z, zp)
        return rcopy(
            part.at[k, zp], inb.at[k, slot], r_send.at[k, zp], r_recv.at[k, slot], below
        )

    def partial(k):
        right = gbuf[k].reshape(members * t_rows, part_width).astype(BF16)
        left = lhs[1 if k < SPLIT else 0]
        part[k] = mm(left, right, 1, 0).reshape(n_z, rows, part_width)

        if lead and k < SPLIT:
            @pl.when(under)
            def _():
                extra = top_g[k].reshape(members * t_rows, part_width).astype(BF16)
                part[k, :n_z - 1] += mm(top_lhs[...], extra, 1, 0).reshape(
                    n_z - 1, rows, part_width
                )

        @pl.when(z == 0)
        def _():
            for zp in reversed(range(1, n_z)):
                block_up(k, zp).start()

        @pl.when(z == highest_of(k))
        def _():
            for zp in range(highest_of(k)):
                block_down(k, zp).start()

    def pass_on(k):
        for step in range(n_z - 1):
            high, low = n_z - 1 - step, step

            @pl.when((z > 0) & (z < high))
            def _():
                arrived(inb.at[k, high], r_recv.at[k, high])
                part[k, high] = part[k, high] + inb[k, high]
                block_up(k, high).start()

            @pl.when((z < highest_of(k)) & (z > low))
            def _():
                arrived(inb.at[k, low], r_recv.at[k, low])
                part[k, low] = part[k, low] + inb[k, low]
                block_down(k, low).start()

    token_total = t_rows * n_seq * m

    def finish(k):
        @pl.when(down)
        def _():
            arrived(inb.at[k, z], r_recv.at[k, z])
            part[k, z] = part[k, z] + inb[k, z]

        @pl.when(z < highest_of(k))
        def _():
            arrived(inb.at[k, n_z], r_recv.at[k, n_z])
            part[k, z] = part[k, z] + inb[k, n_z]

        at = COLUMN_BLOCK[k // SPLIT] * width + k % SPLIT * part_width
        wg_ref[:, at:at + part_width] = part[k, z] * (1.0 / math.sqrt(token_total))

    def head(h):
        return slice(h * dh, (h + 1) * dh)

    loads[0].wait()
    k_s[...] = mm(tok_ref[...], wk[...], 1, 0).astype(BF16)
    loads[1].wait()
    v_s[...] = mm(tok_ref[...], wv[...], 1, 0).astype(BF16)
    for h in range(H):
        sown[0, h] = mm(k_s[:, head(h)], v_s[:, head(h)], 0, 0)
    pl.semaphore_wait(
        barrier, members - 1 + jnp.where(up, 1, 0)
        + jnp.where(top, members, jnp.where(down, 1, 0))
    )
    exchange_copy(0).start()
    gather_start(0, cot_ref[...])

    def on_lead(condition, action):
        if lead:
            pl.when(condition)(action)

    def top_start():
        for copy in top_copies():
            copy.start()

    on_lead(top, top_start)

    loads[2].wait()
    q_s[...] = mm(tok_ref[...], wq[...], 1, 0).astype(BF16)
    lowest, highest = z == 0, z == n_z - 1
    middle = (z > 0) & (z < n_z - 1)

    @pl.when(lowest)
    def _():
        chain(0)

    columns_start(0, tok_ref[...].astype(F32))
    loads[3].wait()
    back_s[...] = mm(cot_ref[...], wo[...], 1, 1)

    @pl.when(middle)
    def _():
        chain(0)

    columns_finish(0)

    causal = lax.broadcasted_iota(jnp.int32, (t_rows, t_rows), 0) >= (
        lax.broadcasted_iota(jnp.int32, (t_rows, t_rows), 1)
    )
    for h in range(H):
        scores = mm(q_s[:, head(h)], k_s[:, head(h)], 1, 1)
        weights = jnp.where(causal, scores, 0.0).astype(BF16)
        attn_s[h] = weights
        mixed_s[:, head(h)] = mm(weights, v_s[:, head(h)], 1, 0)

    @pl.when(highest)
    def _():
        chain(0)

    def top_spread():
        for i in range(SPLIT):
            arrived(top_g.at[i, me], t_recv.at[i, me])
            for copy in reversed(top_gather_copies(i)):
                copy.start()

    on_lead(under, top_spread)
    chain_finish(0, carried_s)
    for h in range(H):
        mixed_s[:, head(h)] += mm(q_s[:, head(h)], carried_s[h], 1, 0)

    mixed = mixed_s[...]
    scale_rows = jnp.sqrt(jnp.mean(mixed * mixed, axis=-1, keepdims=True) + EPSILON)
    normed = mixed / scale_rows
    nb_s[...] = normed.astype(BF16)
    back = back_s[...]
    dm_s[...] = (
        (back - normed * jnp.mean(back * normed, axis=-1, keepdims=True)) / scale_rows
    ).astype(BF16)
    for h in range(H):
        sown[1, h] = mm(q_s[:, head(h)], dm_s[:, head(h)], 0, 0)
    exchange_copy(1).start()
    columns_start(1, nb_s[...].astype(F32))

    @pl.when(highest)
    def _():
        chain(1)
        if lead:
            for copy in top_column_copies():
                copy.start()

    for h in range(H):
        scores = mm(dm_s[:, head(h)], v_s[:, head(h)], 1, 1)
        bs_s[h] = jnp.where(causal, scores, 0.0).astype(BF16)
        dqkv_s[0, :, head(h)] = (
            mm(bs_s[h], k_s[:, head(h)], 1, 0) + mm(dm_s[:, head(h)], carried_s[h], 1, 1)
        ).astype(BF16)
    gather_start(1, dqkv_s[0])

    @pl.when(middle)
    def _():
        chain(1)

    def chunks(matrix):
        return range(matrix * SPLIT, (matrix + 1) * SPLIT)

    def output_chunks():
        columns_finish(1)
        on_lead(under, top_finish)
        for k in chunks(0):
            gather_finish(k)
            partial(k)

    def query_chunks():
        for k in chunks(1):
            gather_finish(k)
            partial(k)

    output_chunks()
    for h in range(H):
        mixed_s[:, head(h)] = mm(bs_s[h], q_s[:, head(h)], 0, 0)
        back_s[:, head(h)] = mm(attn_s[h], dm_s[:, head(h)], 0, 0)

    @pl.when(lowest)
    def _():
        query_chunks()
        chain(1)

    chain_finish(1, later_s)
    for h in range(H):
        dqkv_s[1, :, head(h)] = (
            mixed_s[:, head(h)] + mm(v_s[:, head(h)], later_s[h], 1, 1)
        ).astype(BF16)
    gather_start(2, dqkv_s[1])
    for h in range(H):
        dqkv_s[2, :, head(h)] = (
            back_s[:, head(h)] + mm(k_s[:, head(h)], later_s[h], 1, 0)
        ).astype(BF16)
    gather_start(3, dqkv_s[2])

    @pl.when(z > 0)
    def _():
        query_chunks()

    for k in chunks(0):
        pass_on(k)
    att_ref[...] = mm(nb_s[...], wo[...], 1, 0).astype(BF16)
    dtok = mm(dqkv_s[0], wq[...], 1, 1)
    dtok = dtok + mm(dqkv_s[1], wk[...], 1, 1)
    dtok_ref[...] = (dtok + mm(dqkv_s[2], wv[...], 1, 1)).astype(BF16)
    count = 4 * SPLIT
    for k in range(2 * SPLIT, count):
        gather_finish(k)
        partial(k)
        pass_on(k - SPLIT)
        finish(k - 2 * SPLIT)
    for k in range(count - SPLIT, count):
        pass_on(k)
        finish(k - SPLIT)
    for k in range(count - SPLIT, count):
        finish(k)

    def top_sent():
        for copy in top_copies() + top_column_copies():
            copy.wait_send()

    def under_sent():
        for i in range(SPLIT):
            for copy in top_gather_copies(i) + top_forward_copies(i):
                copy.wait_send()

    on_lead(top, top_sent)
    on_lead(under, under_sent)

    for way in range(2):
        exchange_copy(way).wait_send()
        for copy in column_copies(way):
            copy.wait_send()
        has_in, has_out, _ = ends(way)
        for j in range(half):
            _, side, ahead = chain_copies(way, j)
            pl.when(has_in)(side.wait_send)
            pl.when(has_out)(ahead.wait_send)
    for k in range(count):
        for copy in gather_copies(k) + forward_copies(k):
            copy.wait_send()
        for zp in range(n_z):
            @pl.when((z < zp) | ((z > zp) & (z <= highest_of(k))))
            def _():
                block_up(k, zp).wait_send()


def copy_kernel(count, *refs):
    sources, results, held = refs[:count], refs[count:2 * count], refs[2 * count:3 * count]
    sems = refs[-1]
    loads = [
        pltpu.make_async_copy(sources[i], held[i], sems.at[0, i]) for i in range(count)
    ]
    stores = [
        pltpu.make_async_copy(held[i], results[i], sems.at[1, i]) for i in range(count)
    ]
    for load in loads:
        load.start()
    for load, store in zip(loads, stores):
        load.wait()
        store.start()
    for store in stores:
        store.wait()


def copied(arrays):
    count = len(arrays)
    anywhere = pl.BlockSpec(memory_space=pl.ANY)
    return pl.pallas_call(
        functools.partial(copy_kernel, count),
        out_shape=tuple(jax.ShapeDtypeStruct(a.shape, a.dtype) for a in arrays),
        in_specs=[anywhere] * count,
        out_specs=(anywhere,) * count,
        scratch_shapes=[pltpu.VMEM(a.shape, a.dtype) for a in arrays]
        + [pltpu.SemaphoreType.DMA((2, count))],
    )(*arrays)


def local(n_seq, m, tokens, w_query, w_key, w_value, w_output, out_cotangent):
    _, t_rows, width = tokens.shape
    dh = width // H
    n_z, members = n_seq // 2, 2 * m
    rows = width // (n_seq * m)
    count = 4 * SPLIT
    top_members = members if leads(members) else 1
    vmem, dma = pltpu.VMEM, pltpu.SemaphoreType.DMA
    block = (t_rows, width)
    states = (2, H, dh, dh)
    in_vmem = pl.BlockSpec(memory_space=pltpu.VMEM)
    anywhere = pl.BlockSpec(memory_space=pl.ANY)
    results = pl.pallas_call(
        functools.partial(kernel, n_seq, m),
        out_shape=(
            jax.ShapeDtypeStruct(block, BF16),
            jax.ShapeDtypeStruct(block, BF16),
            jax.ShapeDtypeStruct((rows, 4 * width), F32),
        ),
        in_specs=[in_vmem, in_vmem] + [anywhere] * 4,
        out_specs=(in_vmem,) * 3,
        scratch_shapes=[vmem((width, width), BF16)] * 4
        + [
            vmem(block, BF16),
            vmem(block, BF16),
            vmem(block, BF16),
            vmem((H, t_rows, t_rows), BF16),
            vmem((H, t_rows, t_rows), BF16),
            vmem(block, F32),
            vmem(block, F32),
            vmem((H, dh, dh), BF16),
            vmem((H, dh, dh), BF16),
            vmem(block, BF16),
            vmem(block, BF16),
            vmem((3,) + block, BF16),
            vmem((count, members, t_rows, width // SPLIT), F32),
            vmem((2, n_z, 2, m, rows, t_rows), F32),
            vmem((2, members, n_z, rows, t_rows), F32),
            vmem((2, n_z * rows, members * t_rows), BF16),
            vmem((count, n_z, rows, width // SPLIT), F32),
            vmem((count, n_z + 1, rows, width // SPLIT), F32),
            vmem(states, F32),
            vmem(states, F32),
            vmem(states, F32),
            vmem((2, H // 2, dh, dh), F32),
            dma((4,)),
            dma((count, m)),
            dma((count, m)),
            dma((count, members)),
            dma((2, members)),
            dma((2, members)),
            dma((2,)),
            dma((2,)),
            dma((2, H // 2)),
            dma((2, H // 2)),
            dma((2, H // 2)),
            dma((2, H // 2)),
            dma((count, n_z)),
            dma((count, n_z + 1)),
            vmem((SPLIT, top_members, t_rows, width // SPLIT), F32),
            vmem((top_members, n_z - 1, rows, t_rows), F32),
            vmem(((n_z - 1) * rows, top_members * t_rows), BF16),
            dma((SPLIT,)),
            dma((SPLIT, m)),
            dma((SPLIT, m)),
            dma((SPLIT, members)),
            dma((members,)),
            dma((members,)),
        ],
        compiler_params=pltpu.CompilerParams(
            collective_id=0, has_side_effects=True, vmem_limit_bytes=60 * 2**20
        ),
    )(
        tokens.reshape(block), out_cotangent.reshape(block),
        w_query, w_key, w_value, w_output,
    )
    attended, d_tokens, weight_grads = copied(results)
    return attended.reshape(tokens.shape), d_tokens.reshape(tokens.shape), weight_grads


def solution(mesh):
    batch = P(("groups", "dp"), "seq", None)
    return jax.shard_map(
        functools.partial(local, mesh.shape["seq"], mesh.shape["dp"]),
        mesh=mesh,
        in_specs=(batch, P(), P(), P(), P(), batch),
        out_specs=(batch, batch, P(("groups", "seq", "dp"), None)),
        check_vma=False,
    )
```

```python
import functools
import math

import jax
import jax.numpy as jnp
from jax import lax
from jax.experimental import pallas as pl
from jax.experimental.pallas import tpu as pltpu
from jax.sharding import PartitionSpec as P

H = 8
EPSILON = 1e-05
MESH = pl.DeviceIdType.MESH
F32, BF16 = jnp.float32, jnp.bfloat16
COLUMN_BLOCK = (3, 0, 1, 2)
SPLIT = 1


def mm(a, b, ca, cb):
    return lax.dot_general(a, b, (((ca,), (cb,)), ((), ())), preferred_element_type=F32)


def kernel(
    n_seq, m,
    tok_ref, cot_ref, wq_hbm, wk_hbm, wv_hbm, wo_hbm,
    att_ref, dtok_ref, wg_ref,
    wq, wk, wv, wo,
    q_s, k_s, v_s, attn_s, bs_s, mixed_s, back_s, carried_s, later_s, dm_s, nb_s, dqkv_s,
    gbuf, xt, xland, lhs, part, inb, sown, spart, crecv, csend,
    w_sem, g_send, g_fwd, g_recv, x_send, x_recv, e_send, e_recv,
    c_send, c_recv, p_send, p_recv, r_send, r_recv,
):
    t_rows, width = tok_ref.shape
    dh = width // H
    half = H // 2
    n_z = n_seq // 2
    rows = wg_ref.shape[0]
    members = 2 * m
    s, d = lax.axis_index("seq"), lax.axis_index("dp")
    z, c = lax.div(s, 2), lax.rem(s, 2)
    me = c * m + d
    up, down = z < n_z - 1, z > 0
    partner = {"seq": 2 * z + 1 - c, "dp": d}
    above = {"seq": jnp.minimum(s + 2, n_seq - 2 + c), "dp": d}
    below = {"seq": jnp.maximum(s - 2, c), "dp": d}
    part_width = width // SPLIT

    def rcopy(src, dst, ss, rs, dev):
        return pltpu.make_async_remote_copy(
            src_ref=src, dst_ref=dst, send_sem=ss, recv_sem=rs,
            device_id=dev, device_id_type=MESH,
        )

    def arrived(ref, sem):
        rcopy(ref, ref, w_sem.at[0], sem, partner).wait_recv()

    loads = [
        pltpu.make_async_copy(src, dst, w_sem.at[i])
        for i, (src, dst) in enumerate(
            ((wk_hbm, wk), (wv_hbm, wv), (wq_hbm, wq), (wo_hbm, wo))
        )
    ]
    for load in loads:
        load.start()

    def member(rel):
        t = lax.rem(me + rel, members)
        return t, lax.div(t, m), lax.rem(t, m)

    barrier = pltpu.get_barrier_semaphore()
    for rel in range(1, members):
        _, tc, td = member(rel)
        pl.semaphore_signal(
            barrier, inc=1, device_id={"seq": 2 * z + tc, "dp": td}, device_id_type=MESH
        )

    @pl.when(up)
    def _():
        pl.semaphore_signal(barrier, inc=1, device_id=above, device_id_type=MESH)

    @pl.when(down)
    def _():
        pl.semaphore_signal(barrier, inc=1, device_id=below, device_id_type=MESH)

    def gather_copies(k):
        own = gbuf.at[k, me]
        copies = [rcopy(own, own, g_send.at[k, 0], g_recv.at[k, me], partner)]
        for j in range(1, m):
            to = {"seq": s, "dp": lax.rem(d + j, m)}
            copies.append(rcopy(own, own, g_send.at[k, j], g_recv.at[k, me], to))
        return copies

    def forward_copies(k):
        copies = []
        for j in range(1, m):
            slot = c * m + lax.rem(d + m - j, m)
            ref = gbuf.at[k, slot]
            copies.append(rcopy(ref, ref, g_fwd.at[k, j], g_recv.at[k, slot], partner))
        return copies

    def gather_start(matrix, value):
        for i in range(SPLIT):
            k = matrix * SPLIT + i
            gbuf[k, me] = value[:, i * part_width:(i + 1) * part_width].astype(F32)
            for copy in reversed(gather_copies(k)):
                copy.start()

    def gather_finish(k):
        for copy in forward_copies(k):
            copy.wait_recv()
            copy.start()
        for j in range(m):
            slot = (1 - c) * m + j
            arrived(gbuf.at[k, slot], g_recv.at[k, slot])

    def column_copies(kind):
        copies = []
        for rel in range(1, members):
            t, tc, td = member(rel)
            copies.append(rcopy(
                xt.at[kind, :, tc, td], xland.at[kind, me], x_send.at[kind, rel],
                x_recv.at[kind, me], {"seq": 2 * z + tc, "dp": td},
            ))
        return copies

    def columns_start(kind, value):
        xt[kind] = value.T.reshape(n_z, 2, m, rows, t_rows)
        xland[kind, me] = xt[kind, :, c, d]
        for copy in column_copies(kind):
            copy.start()

    def columns_finish(kind):
        for rel in range(1, members):
            t, _, _ = member(rel)
            arrived(xland.at[kind, t], x_recv.at[kind, t])
        for j in range(members):
            lhs[kind, :, j * t_rows:(j + 1) * t_rows] = (
                xland[kind, j].reshape(n_z * rows, t_rows).astype(BF16)
            )

    def exchange_copy(way):
        return rcopy(sown.at[way], spart.at[way], e_send.at[way], e_recv.at[way], partner)

    def ends(way):
        return (down, up, above) if way == 0 else (up, down, below)

    def chain_copies(way, j):
        h = c * half + j
        ref = crecv.at[way, h]
        side = rcopy(ref, ref, p_send.at[way, j], p_recv.at[way, j], partner)
        ahead = rcopy(
            csend.at[way, j], ref, c_send.at[way, j], c_recv.at[way, j], ends(way)[2]
        )
        return h, side, ahead

    def chain(way):
        has_in, has_out, _ = ends(way)
        arrived(spart.at[way], e_recv.at[way])

        @pl.when(jnp.logical_not(has_in))
        def _():
            crecv[way] = jnp.zeros(crecv.shape[1:], F32)

        for j in range(half):
            h, side, ahead = chain_copies(way, j)

            @pl.when(has_in)
            def _():
                arrived(crecv.at[way, h], c_recv.at[way, j])

            @pl.when(has_out)
            def _():
                csend[way, j] = crecv[way, h] + (sown[way, h] + spart[way, h])
                ahead.start()

            @pl.when(has_in)
            def _():
                side.start()

    def chain_finish(way, out):
        has_in = ends(way)[0]
        for j in range(half):
            @pl.when(has_in)
            def _():
                arrived(crecv.at[way, (1 - c) * half + j], p_recv.at[way, j])

        takes = c == 1 - way
        for h in range(H):
            out[h] = jnp.where(
                takes, crecv[way, h] + spart[way, h], crecv[way, h]
            ).astype(BF16)

    def block_up(k, zp):
        ref = part.at[k, zp]
        return rcopy(ref, inb.at[k, zp], r_send.at[k, zp], r_recv.at[k, zp], above)

    def block_down(k, zp):
        slot = jnp.where(zp == z - 1, n_z, zp)
        return rcopy(
            part.at[k, zp], inb.at[k, slot], r_send.at[k, zp], r_recv.at[k, slot], below
        )

    def partial(k):
        right = gbuf[k].reshape(members * t_rows, part_width).astype(BF16)
        left = lhs[1 if k < SPLIT else 0]
        part[k] = mm(left, right, 1, 0).reshape(n_z, rows, part_width)

        @pl.when(z == 0)
        def _():
            for zp in reversed(range(1, n_z)):
                block_up(k, zp).start()

        @pl.when(z == n_z - 1)
        def _():
            for zp in range(n_z - 1):
                block_down(k, zp).start()

    def pass_on(k):
        for step in range(n_z - 1):
            high, low = n_z - 1 - step, step

            @pl.when((z > 0) & (z < high))
            def _():
                arrived(inb.at[k, high], r_recv.at[k, high])
                part[k, high] = part[k, high] + inb[k, high]
                block_up(k, high).start()

            @pl.when((z < n_z - 1) & (z > low))
            def _():
                arrived(inb.at[k, low], r_recv.at[k, low])
                part[k, low] = part[k, low] + inb[k, low]
                block_down(k, low).start()

    token_total = t_rows * n_seq * m

    def finish(k):
        @pl.when(down)
        def _():
            arrived(inb.at[k, z], r_recv.at[k, z])
            part[k, z] = part[k, z] + inb[k, z]

        @pl.when(up)
        def _():
            arrived(inb.at[k, n_z], r_recv.at[k, n_z])
            part[k, z] = part[k, z] + inb[k, n_z]

        at = COLUMN_BLOCK[k // SPLIT] * width + k % SPLIT * part_width
        wg_ref[:, at:at + part_width] = part[k, z] * (1.0 / math.sqrt(token_total))

    def head(h):
        return slice(h * dh, (h + 1) * dh)

    loads[0].wait()
    k_s[...] = mm(tok_ref[...], wk[...], 1, 0).astype(BF16)
    loads[1].wait()
    v_s[...] = mm(tok_ref[...], wv[...], 1, 0).astype(BF16)
    for h in range(H):
        sown[0, h] = mm(k_s[:, head(h)], v_s[:, head(h)], 0, 0)
    pl.semaphore_wait(
        barrier, members - 1 + jnp.where(up, 1, 0) + jnp.where(down, 1, 0)
    )
    exchange_copy(0).start()
    gather_start(0, cot_ref[...])
    loads[2].wait()
    q_s[...] = mm(tok_ref[...], wq[...], 1, 0).astype(BF16)
    lowest, highest = z == 0, z == n_z - 1
    middle = (z > 0) & (z < n_z - 1)

    @pl.when(lowest)
    def _():
        chain(0)

    columns_start(0, tok_ref[...].astype(F32))
    loads[3].wait()
    back_s[...] = mm(cot_ref[...], wo[...], 1, 1)

    @pl.when(middle)
    def _():
        chain(0)

    causal = lax.broadcasted_iota(jnp.int32, (t_rows, t_rows), 0) >= (
        lax.broadcasted_iota(jnp.int32, (t_rows, t_rows), 1)
    )
    for h in range(H):
        scores = mm(q_s[:, head(h)], k_s[:, head(h)], 1, 1)
        weights = jnp.where(causal, scores, 0.0).astype(BF16)
        attn_s[h] = weights
        mixed_s[:, head(h)] = mm(weights, v_s[:, head(h)], 1, 0)

    @pl.when(highest)
    def _():
        chain(0)

    chain_finish(0, carried_s)
    for h in range(H):
        mixed_s[:, head(h)] += mm(q_s[:, head(h)], carried_s[h], 1, 0)

    mixed = mixed_s[...]
    scale_rows = jnp.sqrt(jnp.mean(mixed * mixed, axis=-1, keepdims=True) + EPSILON)
    normed = mixed / scale_rows
    nb_s[...] = normed.astype(BF16)
    back = back_s[...]
    dm_s[...] = (
        (back - normed * jnp.mean(back * normed, axis=-1, keepdims=True)) / scale_rows
    ).astype(BF16)
    for h in range(H):
        sown[1, h] = mm(q_s[:, head(h)], dm_s[:, head(h)], 0, 0)
    exchange_copy(1).start()
    columns_start(1, nb_s[...].astype(F32))

    @pl.when(highest)
    def _():
        chain(1)

    for h in range(H):
        scores = mm(dm_s[:, head(h)], v_s[:, head(h)], 1, 1)
        bs_s[h] = jnp.where(causal, scores, 0.0).astype(BF16)
        dqkv_s[0, :, head(h)] = (
            mm(bs_s[h], k_s[:, head(h)], 1, 0) + mm(dm_s[:, head(h)], carried_s[h], 1, 1)
        ).astype(BF16)
    gather_start(1, dqkv_s[0])
    for h in range(H):
        mixed_s[:, head(h)] = mm(bs_s[h], q_s[:, head(h)], 0, 0)
        back_s[:, head(h)] = mm(attn_s[h], dm_s[:, head(h)], 0, 0)

    @pl.when(middle)
    def _():
        chain(1)

    def chunks(matrix):
        return range(matrix * SPLIT, (matrix + 1) * SPLIT)

    def output_chunks():
        columns_finish(0)
        columns_finish(1)
        for k in chunks(0):
            gather_finish(k)
            partial(k)

    def query_chunks():
        for k in chunks(1):
            gather_finish(k)
            partial(k)

    @pl.when(jnp.logical_not(middle))
    def _():
        output_chunks()

    @pl.when(lowest)
    def _():
        query_chunks()
        chain(1)

    chain_finish(1, later_s)
    for h in range(H):
        dqkv_s[1, :, head(h)] = (
            mixed_s[:, head(h)] + mm(v_s[:, head(h)], later_s[h], 1, 1)
        ).astype(BF16)
    gather_start(2, dqkv_s[1])
    for h in range(H):
        dqkv_s[2, :, head(h)] = (
            back_s[:, head(h)] + mm(k_s[:, head(h)], later_s[h], 1, 0)
        ).astype(BF16)
    gather_start(3, dqkv_s[2])

    @pl.when(middle)
    def _():
        output_chunks()

    @pl.when(z > 0)
    def _():
        query_chunks()

    for k in chunks(0):
        pass_on(k)
    att_ref[...] = mm(nb_s[...], wo[...], 1, 0).astype(BF16)
    dtok = mm(dqkv_s[0], wq[...], 1, 1)
    dtok = dtok + mm(dqkv_s[1], wk[...], 1, 1)
    dtok_ref[...] = (dtok + mm(dqkv_s[2], wv[...], 1, 1)).astype(BF16)
    count = 4 * SPLIT
    for k in range(2 * SPLIT, count):
        gather_finish(k)
        partial(k)
        pass_on(k - SPLIT)
        finish(k - 2 * SPLIT)
    for k in range(count - SPLIT, count):
        pass_on(k)
        finish(k - SPLIT)
    for k in range(count - SPLIT, count):
        finish(k)

    for way in range(2):
        exchange_copy(way).wait_send()
        for copy in column_copies(way):
            copy.wait_send()
        has_in, has_out, _ = ends(way)
        for j in range(half):
            _, side, ahead = chain_copies(way, j)
            pl.when(has_in)(side.wait_send)
            pl.when(has_out)(ahead.wait_send)
    for k in range(count):
        for copy in gather_copies(k) + forward_copies(k):
            copy.wait_send()
        for zp in range(n_z):
            @pl.when(z != zp)
            def _():
                block_up(k, zp).wait_send()


def copy_kernel(count, *refs):
    sources, results, held = refs[:count], refs[count:2 * count], refs[2 * count:3 * count]
    sems = refs[-1]
    loads = [
        pltpu.make_async_copy(sources[i], held[i], sems.at[0, i]) for i in range(count)
    ]
    stores = [
        pltpu.make_async_copy(held[i], results[i], sems.at[1, i]) for i in range(count)
    ]
    for load in loads:
        load.start()
    for load, store in zip(loads, stores):
        load.wait()
        store.start()
    for store in stores:
        store.wait()


def copied(arrays):
    count = len(arrays)
    anywhere = pl.BlockSpec(memory_space=pl.ANY)
    return pl.pallas_call(
        functools.partial(copy_kernel, count),
        out_shape=tuple(jax.ShapeDtypeStruct(a.shape, a.dtype) for a in arrays),
        in_specs=[anywhere] * count,
        out_specs=(anywhere,) * count,
        scratch_shapes=[pltpu.VMEM(a.shape, a.dtype) for a in arrays]
        + [pltpu.SemaphoreType.DMA((2, count))],
    )(*arrays)


def local(n_seq, m, tokens, w_query, w_key, w_value, w_output, out_cotangent):
    _, t_rows, width = tokens.shape
    dh = width // H
    n_z, members = n_seq // 2, 2 * m
    rows = width // (n_seq * m)
    count = 4 * SPLIT
    vmem, dma = pltpu.VMEM, pltpu.SemaphoreType.DMA
    block = (t_rows, width)
    states = (2, H, dh, dh)
    in_vmem = pl.BlockSpec(memory_space=pltpu.VMEM)
    anywhere = pl.BlockSpec(memory_space=pl.ANY)
    results = pl.pallas_call(
        functools.partial(kernel, n_seq, m),
        out_shape=(
            jax.ShapeDtypeStruct(block, BF16),
            jax.ShapeDtypeStruct(block, BF16),
            jax.ShapeDtypeStruct((rows, 4 * width), F32),
        ),
        in_specs=[in_vmem, in_vmem] + [anywhere] * 4,
        out_specs=(in_vmem,) * 3,
        scratch_shapes=[vmem((width, width), BF16)] * 4
        + [
            vmem(block, BF16),
            vmem(block, BF16),
            vmem(block, BF16),
            vmem((H, t_rows, t_rows), BF16),
            vmem((H, t_rows, t_rows), BF16),
            vmem(block, F32),
            vmem(block, F32),
            vmem((H, dh, dh), BF16),
            vmem((H, dh, dh), BF16),
            vmem(block, BF16),
            vmem(block, BF16),
            vmem((3,) + block, BF16),
            vmem((count, members, t_rows, width // SPLIT), F32),
            vmem((2, n_z, 2, m, rows, t_rows), F32),
            vmem((2, members, n_z, rows, t_rows), F32),
            vmem((2, n_z * rows, members * t_rows), BF16),
            vmem((count, n_z, rows, width // SPLIT), F32),
            vmem((count, n_z + 1, rows, width // SPLIT), F32),
            vmem(states, F32),
            vmem(states, F32),
            vmem(states, F32),
            vmem((2, H // 2, dh, dh), F32),
            dma((4,)),
            dma((count, m)),
            dma((count, m)),
            dma((count, members)),
            dma((2, members)),
            dma((2, members)),
            dma((2,)),
            dma((2,)),
            dma((2, H // 2)),
            dma((2, H // 2)),
            dma((2, H // 2)),
            dma((2, H // 2)),
            dma((count, n_z)),
            dma((count, n_z + 1)),
        ],
        compiler_params=pltpu.CompilerParams(
            collective_id=0, has_side_effects=True, vmem_limit_bytes=60 * 2**20
        ),
    )(
        tokens.reshape(block), out_cotangent.reshape(block),
        w_query, w_key, w_value, w_output,
    )
    attended, d_tokens, weight_grads = copied(results)
    return attended.reshape(tokens.shape), d_tokens.reshape(tokens.shape), weight_grads


def solution(mesh):
    batch = P(("groups", "dp"), "seq", None)
    return jax.shard_map(
        functools.partial(local, mesh.shape["seq"], mesh.shape["dp"]),
        mesh=mesh,
        in_specs=(batch, P(), P(), P(), P(), batch),
        out_specs=(batch, batch, P(("groups", "seq", "dp"), None)),
        check_vma=False,
    )
```

```python
import functools
import math

import jax
import jax.numpy as jnp
from jax import lax
from jax.experimental import pallas as pl
from jax.experimental.pallas import tpu as pltpu
from jax.sharding import PartitionSpec as P

H = 8
EPSILON = 1e-05
MESH = pl.DeviceIdType.MESH
F32, BF16 = jnp.float32, jnp.bfloat16
COLUMN_BLOCK = (3, 0, 1, 2)
SPLIT = 2


def mm(a, b, ca, cb):
    return lax.dot_general(a, b, (((ca,), (cb,)), ((), ())), preferred_element_type=F32)


def kernel(
    n_seq, m,
    tok_ref, cot_ref, wq_hbm, wk_hbm, wv_hbm, wo_hbm,
    att_ref, dtok_ref, wg_ref,
    wq, wk, wv, wo,
    q_s, k_s, v_s, attn_s, bs_s, mixed_s, back_s, carried_s, later_s, dm_s, nb_s, dqkv_s,
    gbuf, xt, xland, lhs, part, inb, sown, spart, crecv, csend,
    w_sem, g_send, g_fwd, g_recv, x_send, x_recv, e_send, e_recv,
    c_send, c_recv, p_send, p_recv, r_send, r_recv,
):
    t_rows, width = tok_ref.shape
    dh = width // H
    half = H // 2
    n_z = n_seq // 2
    rows = wg_ref.shape[0]
    members = 2 * m
    s, d = lax.axis_index("seq"), lax.axis_index("dp")
    z, c = lax.div(s, 2), lax.rem(s, 2)
    me = c * m + d
    up, down = z < n_z - 1, z > 0
    partner = {"seq": 2 * z + 1 - c, "dp": d}
    above = {"seq": jnp.minimum(s + 2, n_seq - 2 + c), "dp": d}
    below = {"seq": jnp.maximum(s - 2, c), "dp": d}
    part_width = width // SPLIT

    def rcopy(src, dst, ss, rs, dev):
        return pltpu.make_async_remote_copy(
            src_ref=src, dst_ref=dst, send_sem=ss, recv_sem=rs,
            device_id=dev, device_id_type=MESH,
        )

    def arrived(ref, sem):
        rcopy(ref, ref, w_sem.at[0], sem, partner).wait_recv()

    loads = [
        pltpu.make_async_copy(src, dst, w_sem.at[i])
        for i, (src, dst) in enumerate(
            ((wk_hbm, wk), (wv_hbm, wv), (wq_hbm, wq), (wo_hbm, wo))
        )
    ]
    for load in loads:
        load.start()

    def member(rel):
        t = lax.rem(me + rel, members)
        return t, lax.div(t, m), lax.rem(t, m)

    barrier = pltpu.get_barrier_semaphore()
    for rel in range(1, members):
        _, tc, td = member(rel)
        pl.semaphore_signal(
            barrier, inc=1, device_id={"seq": 2 * z + tc, "dp": td}, device_id_type=MESH
        )

    @pl.when(up)
    def _():
        pl.semaphore_signal(barrier, inc=1, device_id=above, device_id_type=MESH)

    @pl.when(down)
    def _():
        pl.semaphore_signal(barrier, inc=1, device_id=below, device_id_type=MESH)

    def gather_copies(k):
        own = gbuf.at[k, me]
        copies = [rcopy(own, own, g_send.at[k, 0], g_recv.at[k, me], partner)]
        for j in range(1, m):
            to = {"seq": s, "dp": lax.rem(d + j, m)}
            copies.append(rcopy(own, own, g_send.at[k, j], g_recv.at[k, me], to))
        return copies

    def forward_copies(k):
        copies = []
        for j in range(1, m):
            slot = c * m + lax.rem(d + m - j, m)
            ref = gbuf.at[k, slot]
            copies.append(rcopy(ref, ref, g_fwd.at[k, j], g_recv.at[k, slot], partner))
        return copies

    def gather_start(matrix, value):
        for i in range(SPLIT):
            k = matrix * SPLIT + i
            gbuf[k, me] = value[:, i * part_width:(i + 1) * part_width].astype(F32)
            for copy in reversed(gather_copies(k)):
                copy.start()

    def gather_finish(k):
        for copy in forward_copies(k):
            copy.wait_recv()
            copy.start()
        for j in range(m):
            slot = (1 - c) * m + j
            arrived(gbuf.at[k, slot], g_recv.at[k, slot])

    def column_copies(kind):
        copies = []
        for rel in range(1, members):
            t, tc, td = member(rel)
            copies.append(rcopy(
                xt.at[kind, :, tc, td], xland.at[kind, me], x_send.at[kind, rel],
                x_recv.at[kind, me], {"seq": 2 * z + tc, "dp": td},
            ))
        return copies

    def columns_start(kind, value):
        xt[kind] = value.T.reshape(n_z, 2, m, rows, t_rows)
        xland[kind, me] = xt[kind, :, c, d]
        for copy in column_copies(kind):
            copy.start()

    def columns_finish(kind):
        for rel in range(1, members):
            t, _, _ = member(rel)
            arrived(xland.at[kind, t], x_recv.at[kind, t])
        for j in range(members):
            lhs[kind, :, j * t_rows:(j + 1) * t_rows] = (
                xland[kind, j].reshape(n_z * rows, t_rows).astype(BF16)
            )

    def exchange_copy(way):
        return rcopy(sown.at[way], spart.at[way], e_send.at[way], e_recv.at[way], partner)

    def ends(way):
        return (down, up, above) if way == 0 else (up, down, below)

    def chain_copies(way, j):
        h = c * half + j
        ref = crecv.at[way, h]
        side = rcopy(ref, ref, p_send.at[way, j], p_recv.at[way, j], partner)
        ahead = rcopy(
            csend.at[way, j], ref, c_send.at[way, j], c_recv.at[way, j], ends(way)[2]
        )
        return h, side, ahead

    def chain(way):
        has_in, has_out, _ = ends(way)
        arrived(spart.at[way], e_recv.at[way])

        @pl.when(jnp.logical_not(has_in))
        def _():
            crecv[way] = jnp.zeros(crecv.shape[1:], F32)

        for j in range(half):
            h, side, ahead = chain_copies(way, j)

            @pl.when(has_in)
            def _():
                arrived(crecv.at[way, h], c_recv.at[way, j])

            @pl.when(has_out)
            def _():
                csend[way, j] = crecv[way, h] + (sown[way, h] + spart[way, h])
                ahead.start()

            @pl.when(has_in)
            def _():
                side.start()

    def chain_finish(way, out):
        has_in = ends(way)[0]
        for j in range(half):
            @pl.when(has_in)
            def _():
                arrived(crecv.at[way, (1 - c) * half + j], p_recv.at[way, j])

        takes = c == 1 - way
        for h in range(H):
            out[h] = jnp.where(
                takes, crecv[way, h] + spart[way, h], crecv[way, h]
            ).astype(BF16)

    def block_up(k, zp):
        ref = part.at[k, zp]
        return rcopy(ref, inb.at[k, zp], r_send.at[k, zp], r_recv.at[k, zp], above)

    def block_down(k, zp):
        slot = jnp.where(zp == z - 1, n_z, zp)
        return rcopy(
            part.at[k, zp], inb.at[k, slot], r_send.at[k, zp], r_recv.at[k, slot], below
        )

    def partial(k):
        right = gbuf[k].reshape(members * t_rows, part_width).astype(BF16)
        left = lhs[1 if k < SPLIT else 0]
        part[k] = mm(left, right, 1, 0).reshape(n_z, rows, part_width)

        @pl.when(z == 0)
        def _():
            for zp in reversed(range(1, n_z)):
                block_up(k, zp).start()

        @pl.when(z == n_z - 1)
        def _():
            for zp in range(n_z - 1):
                block_down(k, zp).start()

    def pass_on(k):
        for step in range(n_z - 1):
            high, low = n_z - 1 - step, step

            @pl.when((z > 0) & (z < high))
            def _():
                arrived(inb.at[k, high], r_recv.at[k, high])
                part[k, high] = part[k, high] + inb[k, high]
                block_up(k, high).start()

            @pl.when((z < n_z - 1) & (z > low))
            def _():
                arrived(inb.at[k, low], r_recv.at[k, low])
                part[k, low] = part[k, low] + inb[k, low]
                block_down(k, low).start()

    token_total = t_rows * n_seq * m

    def finish(k):
        @pl.when(down)
        def _():
            arrived(inb.at[k, z], r_recv.at[k, z])
            part[k, z] = part[k, z] + inb[k, z]

        @pl.when(up)
        def _():
            arrived(inb.at[k, n_z], r_recv.at[k, n_z])
            part[k, z] = part[k, z] + inb[k, n_z]

        at = COLUMN_BLOCK[k // SPLIT] * width + k % SPLIT * part_width
        wg_ref[:, at:at + part_width] = part[k, z] * (1.0 / math.sqrt(token_total))

    def head(h):
        return slice(h * dh, (h + 1) * dh)

    loads[0].wait()
    k_s[...] = mm(tok_ref[...], wk[...], 1, 0).astype(BF16)
    loads[1].wait()
    v_s[...] = mm(tok_ref[...], wv[...], 1, 0).astype(BF16)
    for h in range(H):
        sown[0, h] = mm(k_s[:, head(h)], v_s[:, head(h)], 0, 0)
    pl.semaphore_wait(
        barrier, members - 1 + jnp.where(up, 1, 0) + jnp.where(down, 1, 0)
    )
    exchange_copy(0).start()
    gather_start(0, cot_ref[...])
    loads[2].wait()
    q_s[...] = mm(tok_ref[...], wq[...], 1, 0).astype(BF16)
    lowest, highest = z == 0, z == n_z - 1
    middle = (z > 0) & (z < n_z - 1)

    @pl.when(lowest)
    def _():
        chain(0)

    columns_start(0, tok_ref[...].astype(F32))
    loads[3].wait()
    back_s[...] = mm(cot_ref[...], wo[...], 1, 1)

    @pl.when(middle)
    def _():
        chain(0)

    causal = lax.broadcasted_iota(jnp.int32, (t_rows, t_rows), 0) >= (
        lax.broadcasted_iota(jnp.int32, (t_rows, t_rows), 1)
    )
    for h in range(H):
        scores = mm(q_s[:, head(h)], k_s[:, head(h)], 1, 1)
        weights = jnp.where(causal, scores, 0.0).astype(BF16)
        attn_s[h] = weights
        mixed_s[:, head(h)] = mm(weights, v_s[:, head(h)], 1, 0)

    @pl.when(highest)
    def _():
        chain(0)

    chain_finish(0, carried_s)
    for h in range(H):
        mixed_s[:, head(h)] += mm(q_s[:, head(h)], carried_s[h], 1, 0)

    mixed = mixed_s[...]
    scale_rows = jnp.sqrt(jnp.mean(mixed * mixed, axis=-1, keepdims=True) + EPSILON)
    normed = mixed / scale_rows
    nb_s[...] = normed.astype(BF16)
    back = back_s[...]
    dm_s[...] = (
        (back - normed * jnp.mean(back * normed, axis=-1, keepdims=True)) / scale_rows
    ).astype(BF16)
    for h in range(H):
        sown[1, h] = mm(q_s[:, head(h)], dm_s[:, head(h)], 0, 0)
    exchange_copy(1).start()
    columns_start(1, nb_s[...].astype(F32))

    @pl.when(highest)
    def _():
        chain(1)

    for h in range(H):
        scores = mm(dm_s[:, head(h)], v_s[:, head(h)], 1, 1)
        bs_s[h] = jnp.where(causal, scores, 0.0).astype(BF16)
        dqkv_s[0, :, head(h)] = (
            mm(bs_s[h], k_s[:, head(h)], 1, 0) + mm(dm_s[:, head(h)], carried_s[h], 1, 1)
        ).astype(BF16)
    gather_start(1, dqkv_s[0])
    for h in range(H):
        mixed_s[:, head(h)] = mm(bs_s[h], q_s[:, head(h)], 0, 0)
        back_s[:, head(h)] = mm(attn_s[h], dm_s[:, head(h)], 0, 0)

    @pl.when(middle)
    def _():
        chain(1)

    def chunks(matrix):
        return range(matrix * SPLIT, (matrix + 1) * SPLIT)

    def output_chunks():
        columns_finish(0)
        columns_finish(1)
        for k in chunks(0):
            gather_finish(k)
            partial(k)

    def query_chunks():
        for k in chunks(1):
            gather_finish(k)
            partial(k)

    @pl.when(jnp.logical_not(middle))
    def _():
        output_chunks()

    @pl.when(lowest)
    def _():
        query_chunks()
        chain(1)

    chain_finish(1, later_s)
    for h in range(H):
        dqkv_s[1, :, head(h)] = (
            mixed_s[:, head(h)] + mm(v_s[:, head(h)], later_s[h], 1, 1)
        ).astype(BF16)
    gather_start(2, dqkv_s[1])
    for h in range(H):
        dqkv_s[2, :, head(h)] = (
            back_s[:, head(h)] + mm(k_s[:, head(h)], later_s[h], 1, 0)
        ).astype(BF16)
    gather_start(3, dqkv_s[2])

    @pl.when(middle)
    def _():
        output_chunks()

    @pl.when(z > 0)
    def _():
        query_chunks()

    for k in chunks(0):
        pass_on(k)
    att_ref[...] = mm(nb_s[...], wo[...], 1, 0).astype(BF16)
    dtok = mm(dqkv_s[0], wq[...], 1, 1)
    dtok = dtok + mm(dqkv_s[1], wk[...], 1, 1)
    dtok_ref[...] = (dtok + mm(dqkv_s[2], wv[...], 1, 1)).astype(BF16)
    count = 4 * SPLIT
    for k in range(2 * SPLIT, count):
        gather_finish(k)
        partial(k)
        pass_on(k - SPLIT)
        finish(k - 2 * SPLIT)
    for k in range(count - SPLIT, count):
        pass_on(k)
        finish(k - SPLIT)
    for k in range(count - SPLIT, count):
        finish(k)

    for way in range(2):
        exchange_copy(way).wait_send()
        for copy in column_copies(way):
            copy.wait_send()
        has_in, has_out, _ = ends(way)
        for j in range(half):
            _, side, ahead = chain_copies(way, j)
            pl.when(has_in)(side.wait_send)
            pl.when(has_out)(ahead.wait_send)
    for k in range(count):
        for copy in gather_copies(k) + forward_copies(k):
            copy.wait_send()
        for zp in range(n_z):
            @pl.when(z != zp)
            def _():
                block_up(k, zp).wait_send()


def copy_kernel(count, *refs):
    sources, results, held = refs[:count], refs[count:2 * count], refs[2 * count:3 * count]
    sems = refs[-1]
    loads = [
        pltpu.make_async_copy(sources[i], held[i], sems.at[0, i]) for i in range(count)
    ]
    stores = [
        pltpu.make_async_copy(held[i], results[i], sems.at[1, i]) for i in range(count)
    ]
    for load in loads:
        load.start()
    for load, store in zip(loads, stores):
        load.wait()
        store.start()
    for store in stores:
        store.wait()


def copied(arrays):
    count = len(arrays)
    anywhere = pl.BlockSpec(memory_space=pl.ANY)
    return pl.pallas_call(
        functools.partial(copy_kernel, count),
        out_shape=tuple(jax.ShapeDtypeStruct(a.shape, a.dtype) for a in arrays),
        in_specs=[anywhere] * count,
        out_specs=(anywhere,) * count,
        scratch_shapes=[pltpu.VMEM(a.shape, a.dtype) for a in arrays]
        + [pltpu.SemaphoreType.DMA((2, count))],
    )(*arrays)


def local(n_seq, m, tokens, w_query, w_key, w_value, w_output, out_cotangent):
    _, t_rows, width = tokens.shape
    dh = width // H
    n_z, members = n_seq // 2, 2 * m
    rows = width // (n_seq * m)
    count = 4 * SPLIT
    vmem, dma = pltpu.VMEM, pltpu.SemaphoreType.DMA
    block = (t_rows, width)
    states = (2, H, dh, dh)
    in_vmem = pl.BlockSpec(memory_space=pltpu.VMEM)
    anywhere = pl.BlockSpec(memory_space=pl.ANY)
    results = pl.pallas_call(
        functools.partial(kernel, n_seq, m),
        out_shape=(
            jax.ShapeDtypeStruct(block, BF16),
            jax.ShapeDtypeStruct(block, BF16),
            jax.ShapeDtypeStruct((rows, 4 * width), F32),
        ),
        in_specs=[in_vmem, in_vmem] + [anywhere] * 4,
        out_specs=(in_vmem,) * 3,
        scratch_shapes=[vmem((width, width), BF16)] * 4
        + [
            vmem(block, BF16),
            vmem(block, BF16),
            vmem(block, BF16),
            vmem((H, t_rows, t_rows), BF16),
            vmem((H, t_rows, t_rows), BF16),
            vmem(block, F32),
            vmem(block, F32),
            vmem((H, dh, dh), BF16),
            vmem((H, dh, dh), BF16),
            vmem(block, BF16),
            vmem(block, BF16),
            vmem((3,) + block, BF16),
            vmem((count, members, t_rows, width // SPLIT), F32),
            vmem((2, n_z, 2, m, rows, t_rows), F32),
            vmem((2, members, n_z, rows, t_rows), F32),
            vmem((2, n_z * rows, members * t_rows), BF16),
            vmem((count, n_z, rows, width // SPLIT), F32),
            vmem((count, n_z + 1, rows, width // SPLIT), F32),
            vmem(states, F32),
            vmem(states, F32),
            vmem(states, F32),
            vmem((2, H // 2, dh, dh), F32),
            dma((4,)),
            dma((count, m)),
            dma((count, m)),
            dma((count, members)),
            dma((2, members)),
            dma((2, members)),
            dma((2,)),
            dma((2,)),
            dma((2, H // 2)),
            dma((2, H // 2)),
            dma((2, H // 2)),
            dma((2, H // 2)),
            dma((count, n_z)),
            dma((count, n_z + 1)),
        ],
        compiler_params=pltpu.CompilerParams(
            collective_id=0, has_side_effects=True, vmem_limit_bytes=60 * 2**20
        ),
    )(
        tokens.reshape(block), out_cotangent.reshape(block),
        w_query, w_key, w_value, w_output,
    )
    attended, d_tokens, weight_grads = copied(results)
    return attended.reshape(tokens.shape), d_tokens.reshape(tokens.shape), weight_grads


def solution(mesh):
    batch = P(("groups", "dp"), "seq", None)
    return jax.shard_map(
        functools.partial(local, mesh.shape["seq"], mesh.shape["dp"]),
        mesh=mesh,
        in_specs=(batch, P(), P(), P(), P(), batch),
        out_specs=(batch, batch, P(("groups", "seq", "dp"), None)),
        check_vma=False,
    )
```

```python
import functools
import math

import jax
import jax.numpy as jnp
from jax import lax
from jax.experimental import pallas as pl
from jax.experimental.pallas import tpu as pltpu
from jax.sharding import PartitionSpec as P

H = 8
EPSILON = 1e-05
MESH = pl.DeviceIdType.MESH
F32, BF16 = jnp.float32, jnp.bfloat16
COLUMN_BLOCK = (3, 0, 1, 2)
SPLIT = 1


def mm(a, b, ca, cb):
    return lax.dot_general(a, b, (((ca,), (cb,)), ((), ())), preferred_element_type=F32)


def kernel(
    n_seq, m,
    tok_ref, cot_ref, wq_hbm, wk_hbm, wv_hbm, wo_hbm,
    att_ref, dtok_ref, wg_ref,
    wq, wk, wv, wo,
    q_s, k_s, v_s, attn_s, bs_s, mixed_s, back_s, carried_s, later_s, dm_s, nb_s, dqkv_s,
    gbuf, xt, xland, lhs, part, inb, sown, spart, crecv, csend,
    w_sem, g_send, g_fwd, g_recv, x_send, x_recv, e_send, e_recv,
    c_send, c_recv, p_send, p_recv, r_send, r_recv,
):
    t_rows, width = tok_ref.shape
    dh = width // H
    half = H // 2
    n_z = n_seq // 2
    rows = wg_ref.shape[0]
    members = 2 * m
    s, d = lax.axis_index("seq"), lax.axis_index("dp")
    z, c = lax.div(s, 2), lax.rem(s, 2)
    me = c * m + d
    up, down = z < n_z - 1, z > 0
    partner = {"seq": 2 * z + 1 - c, "dp": d}
    above = {"seq": jnp.minimum(s + 2, n_seq - 2 + c), "dp": d}
    below = {"seq": jnp.maximum(s - 2, c), "dp": d}
    part_width = width // SPLIT

    def rcopy(src, dst, ss, rs, dev):
        return pltpu.make_async_remote_copy(
            src_ref=src, dst_ref=dst, send_sem=ss, recv_sem=rs,
            device_id=dev, device_id_type=MESH,
        )

    def arrived(ref, sem):
        rcopy(ref, ref, w_sem.at[0], sem, partner).wait_recv()

    loads = [
        pltpu.make_async_copy(src, dst, w_sem.at[i])
        for i, (src, dst) in enumerate(
            ((wk_hbm, wk), (wv_hbm, wv), (wq_hbm, wq), (wo_hbm, wo))
        )
    ]
    for load in loads:
        load.start()

    def member(rel):
        t = lax.rem(me + rel, members)
        return t, lax.div(t, m), lax.rem(t, m)

    barrier = pltpu.get_barrier_semaphore()
    for rel in range(1, members):
        _, tc, td = member(rel)
        pl.semaphore_signal(
            barrier, inc=1, device_id={"seq": 2 * z + tc, "dp": td}, device_id_type=MESH
        )

    @pl.when(up)
    def _():
        pl.semaphore_signal(barrier, inc=1, device_id=above, device_id_type=MESH)

    @pl.when(down)
    def _():
        pl.semaphore_signal(barrier, inc=1, device_id=below, device_id_type=MESH)

    def gather_copies(k):
        own = gbuf.at[k, me]
        copies = [rcopy(own, own, g_send.at[k, 0], g_recv.at[k, me], partner)]
        for j in range(1, m):
            to = {"seq": s, "dp": lax.rem(d + j, m)}
            copies.append(rcopy(own, own, g_send.at[k, j], g_recv.at[k, me], to))
        return copies

    def forward_copies(k):
        copies = []
        for j in range(1, m):
            slot = c * m + lax.rem(d + m - j, m)
            ref = gbuf.at[k, slot]
            copies.append(rcopy(ref, ref, g_fwd.at[k, j], g_recv.at[k, slot], partner))
        return copies

    def gather_start(matrix, value):
        for i in range(SPLIT):
            k = matrix * SPLIT + i
            gbuf[k, me] = value[:, i * part_width:(i + 1) * part_width].astype(F32)
            for copy in reversed(gather_copies(k)):
                copy.start()

    def gather_finish(k):
        for copy in forward_copies(k):
            copy.wait_recv()
            copy.start()
        for j in range(m):
            slot = (1 - c) * m + j
            arrived(gbuf.at[k, slot], g_recv.at[k, slot])

    def column_copies(kind):
        copies = []
        for rel in range(1, members):
            t, tc, td = member(rel)
            copies.append(rcopy(
                xt.at[kind, :, tc, td], xland.at[kind, me], x_send.at[kind, rel],
                x_recv.at[kind, me], {"seq": 2 * z + tc, "dp": td},
            ))
        return copies

    def columns_start(kind, value):
        xt[kind] = value.T.reshape(n_z, 2, m, rows, t_rows)
        xland[kind, me] = xt[kind, :, c, d]
        for copy in column_copies(kind):
            copy.start()

    def columns_finish(kind):
        for rel in range(1, members):
            t, _, _ = member(rel)
            arrived(xland.at[kind, t], x_recv.at[kind, t])
        for j in range(members):
            lhs[kind, :, j * t_rows:(j + 1) * t_rows] = (
                xland[kind, j].reshape(n_z * rows, t_rows).astype(BF16)
            )

    def exchange_copy(way):
        return rcopy(sown.at[way], spart.at[way], e_send.at[way], e_recv.at[way], partner)

    def ends(way):
        return (down, up, above) if way == 0 else (up, down, below)

    def chain_copies(way, j):
        h = c * half + j
        ref = crecv.at[way, h]
        side = rcopy(ref, ref, p_send.at[way, j], p_recv.at[way, j], partner)
        ahead = rcopy(
            csend.at[way, j], ref, c_send.at[way, j], c_recv.at[way, j], ends(way)[2]
        )
        return h, side, ahead

    def chain(way):
        has_in, has_out, _ = ends(way)
        arrived(spart.at[way], e_recv.at[way])

        @pl.when(jnp.logical_not(has_in))
        def _():
            crecv[way] = jnp.zeros(crecv.shape[1:], F32)

        for j in range(half):
            h, side, ahead = chain_copies(way, j)

            @pl.when(has_in)
            def _():
                arrived(crecv.at[way, h], c_recv.at[way, j])

            @pl.when(has_out)
            def _():
                csend[way, j] = crecv[way, h] + (sown[way, h] + spart[way, h])
                ahead.start()

            @pl.when(has_in)
            def _():
                side.start()

    def chain_finish(way, out):
        has_in = ends(way)[0]
        for j in range(half):
            @pl.when(has_in)
            def _():
                arrived(crecv.at[way, (1 - c) * half + j], p_recv.at[way, j])

        takes = c == 1 - way
        for h in range(H):
            out[h] = jnp.where(
                takes, crecv[way, h] + spart[way, h], crecv[way, h]
            ).astype(BF16)

    def block_up(k, zp):
        ref = part.at[k, zp]
        return rcopy(ref, inb.at[k, zp], r_send.at[k, zp], r_recv.at[k, zp], above)

    def block_down(k, zp):
        slot = jnp.where(zp == z - 1, n_z, zp)
        return rcopy(
            part.at[k, zp], inb.at[k, slot], r_send.at[k, zp], r_recv.at[k, slot], below
        )

    def partial(k):
        right = gbuf[k].reshape(members * t_rows, part_width).astype(BF16)
        left = lhs[1 if k < SPLIT else 0]
        part[k] = mm(left, right, 1, 0).reshape(n_z, rows, part_width)

        @pl.when(z == 0)
        def _():
            for zp in reversed(range(1, n_z)):
                block_up(k, zp).start()

        @pl.when(z == n_z - 1)
        def _():
            for zp in range(n_z - 1):
                block_down(k, zp).start()

    def pass_up(k):
        for high in reversed(range(1, n_z)):
            @pl.when((z > 0) & (z < high))
            def _():
                arrived(inb.at[k, high], r_recv.at[k, high])
                part[k, high] = part[k, high] + inb[k, high]
                block_up(k, high).start()

    def pass_down(k):
        for low in range(n_z - 1):
            @pl.when((z < n_z - 1) & (z > low))
            def _():
                arrived(inb.at[k, low], r_recv.at[k, low])
                part[k, low] = part[k, low] + inb[k, low]
                block_down(k, low).start()

    lower = z < n_z // 2

    def pass_on(near, far):
        @pl.when(lower)
        def _():
            if near is not None:
                pass_up(near)
            if far is not None:
                pass_down(far)

        @pl.when(jnp.logical_not(lower))
        def _():
            if near is not None:
                pass_down(near)
            if far is not None:
                pass_up(far)

    token_total = t_rows * n_seq * m

    def finish(k):
        @pl.when(down)
        def _():
            arrived(inb.at[k, z], r_recv.at[k, z])
            part[k, z] = part[k, z] + inb[k, z]

        @pl.when(up)
        def _():
            arrived(inb.at[k, n_z], r_recv.at[k, n_z])
            part[k, z] = part[k, z] + inb[k, n_z]

        at = COLUMN_BLOCK[k // SPLIT] * width + k % SPLIT * part_width
        wg_ref[:, at:at + part_width] = part[k, z] * (1.0 / math.sqrt(token_total))

    def head(h):
        return slice(h * dh, (h + 1) * dh)

    loads[0].wait()
    k_s[...] = mm(tok_ref[...], wk[...], 1, 0).astype(BF16)
    loads[1].wait()
    v_s[...] = mm(tok_ref[...], wv[...], 1, 0).astype(BF16)
    for h in range(H):
        sown[0, h] = mm(k_s[:, head(h)], v_s[:, head(h)], 0, 0)
    pl.semaphore_wait(
        barrier, members - 1 + jnp.where(up, 1, 0) + jnp.where(down, 1, 0)
    )
    exchange_copy(0).start()
    gather_start(0, cot_ref[...])
    loads[2].wait()
    q_s[...] = mm(tok_ref[...], wq[...], 1, 0).astype(BF16)
    lowest, highest = z == 0, z == n_z - 1
    middle = (z > 0) & (z < n_z - 1)

    @pl.when(lowest)
    def _():
        chain(0)

    columns_start(0, tok_ref[...].astype(F32))
    loads[3].wait()
    back_s[...] = mm(cot_ref[...], wo[...], 1, 1)

    @pl.when(middle)
    def _():
        chain(0)

    causal = lax.broadcasted_iota(jnp.int32, (t_rows, t_rows), 0) >= (
        lax.broadcasted_iota(jnp.int32, (t_rows, t_rows), 1)
    )
    for h in range(H):
        scores = mm(q_s[:, head(h)], k_s[:, head(h)], 1, 1)
        weights = jnp.where(causal, scores, 0.0).astype(BF16)
        attn_s[h] = weights
        mixed_s[:, head(h)] = mm(weights, v_s[:, head(h)], 1, 0)

    @pl.when(highest)
    def _():
        chain(0)

    chain_finish(0, carried_s)
    for h in range(H):
        mixed_s[:, head(h)] += mm(q_s[:, head(h)], carried_s[h], 1, 0)

    mixed = mixed_s[...]
    scale_rows = jnp.sqrt(jnp.mean(mixed * mixed, axis=-1, keepdims=True) + EPSILON)
    normed = mixed / scale_rows
    nb_s[...] = normed.astype(BF16)
    back = back_s[...]
    dm_s[...] = (
        (back - normed * jnp.mean(back * normed, axis=-1, keepdims=True)) / scale_rows
    ).astype(BF16)
    for h in range(H):
        sown[1, h] = mm(q_s[:, head(h)], dm_s[:, head(h)], 0, 0)
    exchange_copy(1).start()
    columns_start(1, nb_s[...].astype(F32))

    @pl.when(highest)
    def _():
        chain(1)

    for h in range(H):
        scores = mm(dm_s[:, head(h)], v_s[:, head(h)], 1, 1)
        bs_s[h] = jnp.where(causal, scores, 0.0).astype(BF16)
        dqkv_s[0, :, head(h)] = (
            mm(bs_s[h], k_s[:, head(h)], 1, 0) + mm(dm_s[:, head(h)], carried_s[h], 1, 1)
        ).astype(BF16)
    gather_start(1, dqkv_s[0])
    for h in range(H):
        mixed_s[:, head(h)] = mm(bs_s[h], q_s[:, head(h)], 0, 0)
        back_s[:, head(h)] = mm(attn_s[h], dm_s[:, head(h)], 0, 0)

    @pl.when(middle)
    def _():
        chain(1)

    def chunks(matrix):
        return range(matrix * SPLIT, (matrix + 1) * SPLIT)

    def output_chunks():
        columns_finish(0)
        columns_finish(1)
        for k in chunks(0):
            gather_finish(k)
            partial(k)

    def query_chunks():
        for k in chunks(1):
            gather_finish(k)
            partial(k)

    @pl.when(jnp.logical_not(middle))
    def _():
        output_chunks()

    @pl.when(lowest)
    def _():
        query_chunks()
        chain(1)

    chain_finish(1, later_s)
    for h in range(H):
        dqkv_s[1, :, head(h)] = (
            mixed_s[:, head(h)] + mm(v_s[:, head(h)], later_s[h], 1, 1)
        ).astype(BF16)
    gather_start(2, dqkv_s[1])
    for h in range(H):
        dqkv_s[2, :, head(h)] = (
            back_s[:, head(h)] + mm(k_s[:, head(h)], later_s[h], 1, 0)
        ).astype(BF16)
    gather_start(3, dqkv_s[2])

    @pl.when(middle)
    def _():
        output_chunks()

    pass_on(0, None)

    @pl.when(z > 0)
    def _():
        query_chunks()

    pass_on(1, 0)
    dtok = mm(dqkv_s[0], wq[...], 1, 1)
    dtok = dtok + mm(dqkv_s[1], wk[...], 1, 1)
    dtok_ref[...] = (dtok + mm(dqkv_s[2], wv[...], 1, 1)).astype(BF16)
    gather_finish(2)
    partial(2)
    pass_on(2, 1)
    att_ref[...] = mm(nb_s[...], wo[...], 1, 0).astype(BF16)
    gather_finish(3)
    partial(3)
    pass_on(3, 2)
    pass_on(None, 3)
    count = 4 * SPLIT
    for k in range(count):
        finish(k)

    for way in range(2):
        exchange_copy(way).wait_send()
        for copy in column_copies(way):
            copy.wait_send()
        has_in, has_out, _ = ends(way)
        for j in range(half):
            _, side, ahead = chain_copies(way, j)
            pl.when(has_in)(side.wait_send)
            pl.when(has_out)(ahead.wait_send)
    for k in range(count):
        for copy in gather_copies(k) + forward_copies(k):
            copy.wait_send()
        for zp in range(n_z):
            @pl.when(z != zp)
            def _():
                block_up(k, zp).wait_send()


def copy_kernel(count, *refs):
    sources, results, held = refs[:count], refs[count:2 * count], refs[2 * count:3 * count]
    sems = refs[-1]
    loads = [
        pltpu.make_async_copy(sources[i], held[i], sems.at[0, i]) for i in range(count)
    ]
    stores = [
        pltpu.make_async_copy(held[i], results[i], sems.at[1, i]) for i in range(count)
    ]
    for load in loads:
        load.start()
    for load, store in zip(loads, stores):
        load.wait()
        store.start()
    for store in stores:
        store.wait()


def copied(arrays):
    count = len(arrays)
    anywhere = pl.BlockSpec(memory_space=pl.ANY)
    return pl.pallas_call(
        functools.partial(copy_kernel, count),
        out_shape=tuple(jax.ShapeDtypeStruct(a.shape, a.dtype) for a in arrays),
        in_specs=[anywhere] * count,
        out_specs=(anywhere,) * count,
        scratch_shapes=[pltpu.VMEM(a.shape, a.dtype) for a in arrays]
        + [pltpu.SemaphoreType.DMA((2, count))],
    )(*arrays)


def local(n_seq, m, tokens, w_query, w_key, w_value, w_output, out_cotangent):
    _, t_rows, width = tokens.shape
    dh = width // H
    n_z, members = n_seq // 2, 2 * m
    rows = width // (n_seq * m)
    count = 4 * SPLIT
    vmem, dma = pltpu.VMEM, pltpu.SemaphoreType.DMA
    block = (t_rows, width)
    states = (2, H, dh, dh)
    in_vmem = pl.BlockSpec(memory_space=pltpu.VMEM)
    anywhere = pl.BlockSpec(memory_space=pl.ANY)
    results = pl.pallas_call(
        functools.partial(kernel, n_seq, m),
        out_shape=(
            jax.ShapeDtypeStruct(block, BF16),
            jax.ShapeDtypeStruct(block, BF16),
            jax.ShapeDtypeStruct((rows, 4 * width), F32),
        ),
        in_specs=[in_vmem, in_vmem] + [anywhere] * 4,
        out_specs=(in_vmem,) * 3,
        scratch_shapes=[vmem((width, width), BF16)] * 4
        + [
            vmem(block, BF16),
            vmem(block, BF16),
            vmem(block, BF16),
            vmem((H, t_rows, t_rows), BF16),
            vmem((H, t_rows, t_rows), BF16),
            vmem(block, F32),
            vmem(block, F32),
            vmem((H, dh, dh), BF16),
            vmem((H, dh, dh), BF16),
            vmem(block, BF16),
            vmem(block, BF16),
            vmem((3,) + block, BF16),
            vmem((count, members, t_rows, width // SPLIT), F32),
            vmem((2, n_z, 2, m, rows, t_rows), F32),
            vmem((2, members, n_z, rows, t_rows), F32),
            vmem((2, n_z * rows, members * t_rows), BF16),
            vmem((count, n_z, rows, width // SPLIT), F32),
            vmem((count, n_z + 1, rows, width // SPLIT), F32),
            vmem(states, F32),
            vmem(states, F32),
            vmem(states, F32),
            vmem((2, H // 2, dh, dh), F32),
            dma((4,)),
            dma((count, m)),
            dma((count, m)),
            dma((count, members)),
            dma((2, members)),
            dma((2, members)),
            dma((2,)),
            dma((2,)),
            dma((2, H // 2)),
            dma((2, H // 2)),
            dma((2, H // 2)),
            dma((2, H // 2)),
            dma((count, n_z)),
            dma((count, n_z + 1)),
        ],
        compiler_params=pltpu.CompilerParams(
            collective_id=0, has_side_effects=True, vmem_limit_bytes=60 * 2**20
        ),
    )(
        tokens.reshape(block), out_cotangent.reshape(block),
        w_query, w_key, w_value, w_output,
    )
    attended, d_tokens, weight_grads = copied(results)
    return attended.reshape(tokens.shape), d_tokens.reshape(tokens.shape), weight_grads


def solution(mesh):
    batch = P(("groups", "dp"), "seq", None)
    return jax.shard_map(
        functools.partial(local, mesh.shape["seq"], mesh.shape["dp"]),
        mesh=mesh,
        in_specs=(batch, P(), P(), P(), P(), batch),
        out_specs=(batch, batch, P(("groups", "seq", "dp"), None)),
        check_vma=False,
    )
```
